512 devices in a mesh: rep: 64 (over z, y_lo, core), tp: 8 (over y_hi, x).
Axes of the slice: x: 4, y: 4 (y_hi: 2, y_lo: 2; y = y_hi * 2 + y_lo), z: 16, core: 2. Of those that a mesh axis runs over, the one named last changes fastest.
Arguments:
- hidden_rows: bfloat16 [64, 2, 256, 2048], P('rep', None, 'tp'), may hold values from -6 to 6
- query_heads: bfloat16 [64, 2, 256, 2048], P('rep', None, None, 'tp'), may hold values from -6 to 6
- key_heads: bfloat16 [64, 2, 256, 2048], P('rep', None, None, 'tp'), may hold values from -6 to 6
- teacher_out: bfloat16 [64, 2, 256, 2048], P('rep', None, None, 'tp'), may hold values from -6 to 6
- segment_ids: int32 [64, 2, 256], P('rep'), may hold values from 0 to 7, never falling along the last dimension, each value on 1 to 64 neighbouring positions
- prompt_lens: int32 [64, 2, 8], P('rep'), may hold values from 0 to 31
- gossip_step: int32 [1], replicated, may hold values from 0 to 63
- value_weight: bfloat16 [64, 2048, 2048], P('rep', None, 'tp'), may hold values from -0.125 to 0.125
- momentum: bfloat16 [64, 2048, 2048], P('rep', None, 'tp'), may hold values from -0.29882812 to 0.29882812
Outputs:
- new_weight: bfloat16 [64, 2048, 2048], P('rep', None, 'tp')
- new_momentum: bfloat16 [64, 2048, 2048], P('rep', None, 'tp')
The draws below stay inside these ranges and needn't reach their ends.
Inputs may be any that keep to these rules, and one draw needn't show every extreme that they name: `segment_ids`: ids never fall along the 256 positions; each microbatch holds 1 to 64 positions, and one of each pack exactly 64. `gossip_step`: the same for every replica.
All inputs are finite; a program needn't handle non-finite values.
Results may differ from the reference program's by a relative error of at most 0.013.
Values may be sent and summed in bfloat16 or wider, within the bound.
A program may use at most 64 MiB of HBM per device.

```python
import math
import jax
import jax.numpy as jnp
import numpy as np
from jax import lax

D = 2048
HEADS = 16
HEAD_DIM = 128
TOK = 256
STEPS = 2
SEGS = 8
SEG_MOST = 64
REPS = 64
N_REP = 64


def draw_query_heads(key, part):
    key = jax.random.fold_in(key, 7)
    full_shape = (REPS, STEPS, TOK, HEADS * HEAD_DIM)
    normal_draw = jnp.clip(jax.random.normal(key, full_shape, jnp.float32), -6.0, 6.0)
    return normal_draw.astype(jnp.bfloat16)


def draw_key_heads(key, part):
    key = jax.random.fold_in(key, 13)
    full_shape = (REPS, STEPS, TOK, HEADS * HEAD_DIM)
    normal_draw = jnp.clip(jax.random.normal(key, full_shape, jnp.float32), -6.0, 6.0)
    return normal_draw.astype(jnp.bfloat16)


def plant(array, rng, smallest, high):
    dims = array.shape
    place = [jax.random.randint(jax.random.fold_in(rng, axis), (), 0, dims[axis]) for axis in range(len(dims))]
    array = array.at[tuple(place)].set(smallest)
    longest = dims.index(max(dims))
    place[longest] = (place[longest] + 1) % dims[longest]
    return array.at[tuple(place)].set(high)


def block_scale(key, dims, cuts, low, top_value):
    level = 1.0
    for position, parts in cuts:
        draws = jax.random.uniform(jax.random.fold_in(jax.random.fold_in(key, 6), position), (parts,), jnp.float32, low / len(cuts), top_value / len(cuts))
        level = level * jnp.repeat(jnp.exp(draws), dims[position] // parts).reshape((-1,) + (1,) * (len(dims) - 1 - position))
    return level


def profile(count, total, reach, lean):
    portions = [(1 << 20) // math.isqrt(standing ** lean) + 1 for standing in range(2, count + 1)]
    rest, counts = total - reach - (count - 1), [1] * (count - 1)
    while rest > 0:
        movable = [i for i in range(count - 1) if counts[i] < reach]
        pool, left = sum([portions[i] for i in movable]), rest
        for i in movable:
            addition = min(reach - counts[i], max(1, left * portions[i] // pool), rest)
            counts[i] = counts[i] + addition
            rest = rest - addition
    return np.array([reach] + counts)


def uneven_parts(key, count, total, limit, slope):
    if count == 2:
        one = jax.random.randint(key, (), max(1, total - limit), min(limit, total - 1) + 1)
        return jnp.stack([one, total - one])
    lengths = jnp.asarray(profile(count, total, limit, slope), jnp.int32)
    pairs = (count - 1) // 2
    donor, taker = lengths[1:1 + 2 * pairs:2], lengths[2:2 + 2 * pairs:2]
    slack = jnp.minimum(donor - 1, limit - taker)
    shifted = jax.random.randint(jax.random.fold_in(key, 1), (pairs,), 0, 1 << 20) % (slack + 1)
    lengths = lengths.at[1:1 + 2 * pairs:2].set(donor - shifted).at[2:2 + 2 * pairs:2].set(taker + shifted)
    return lengths[jax.random.permutation(jax.random.fold_in(key, 2), count)]


def bell_draw(rng, shape, deviation, bound, pieces=(), kind=jnp.bfloat16):
    values = jax.random.normal(rng, shape, jnp.float32) * deviation
    if len(pieces) > 0:
        values = block_scale(rng, shape, pieces, -0.22, 0.18) * values
    return jnp.clip(values, min=-bound, max=bound).astype(kind)


def setup_inputs(seed: int = 0) -> dict:
    key_of = jax.random.split(jax.random.key(seed), 10)
    hidden_rows = bell_draw(key_of[0], (REPS, STEPS, TOK, D), 1.0, 6.0, ((0, 64), (2, 8)))
    query_heads = draw_query_heads(jax.random.fold_in(key_of[9], 71), 0)
    key_heads = draw_key_heads(jax.random.fold_in(key_of[9], 71), 0)
    teacher_out = bell_draw(key_of[3], (REPS, STEPS, TOK, HEADS * HEAD_DIM), 1.0, 6.0, ((0, 64), (3, 8)))
    segment_ids = jax.vmap(lambda own: jnp.searchsorted(jnp.cumsum(uneven_parts(own, SEGS, TOK, SEG_MOST, 2)), jnp.arange(TOK), side="right"))(jax.random.split(key_of[4], REPS * STEPS)).reshape((REPS, STEPS, TOK)).astype(jnp.int32)
    prompt_lens = plant(jax.random.randint(key_of[5], (REPS, STEPS, SEGS), 0, SEG_MOST // 2), jax.random.fold_in(key_of[5], 1), 0, (SEG_MOST // 2) - 1).astype(jnp.int32)
    gossip_step = jax.random.randint(key_of[6], (1,), 0, 64).astype(jnp.int32)
    value_weight = bell_draw(key_of[7], (REPS, D, HEADS * HEAD_DIM), D ** -0.5, 0.125, ((0, 64), (2, 8)))
    momentum = bell_draw(key_of[8], (REPS, D, HEADS * HEAD_DIM), 0.05, 0.29882812, ((0, 64), (2, 8)))
    return {"hidden_rows": hidden_rows, "query_heads": query_heads, "key_heads": key_heads, "teacher_out": teacher_out, "segment_ids": segment_ids, "prompt_lens": prompt_lens, "gossip_step": gossip_step, "value_weight": value_weight, "momentum": momentum}


LEARN_RATE = 0.1
MOMENTUM_DECAY = 0.9

def loss_layout(segment_row, prompt_row):
    places = jnp.arange(segment_row.shape[0], dtype=jnp.int32)
    same_segment = segment_row[:, None] == segment_row[None, :]
    allowed = same_segment & (places[None, :] <= places[:, None])
    earlier = lax.optimization_barrier(jnp.sum((same_segment & (places[None, :] < places[:, None])).astype(jnp.int32), axis=1))
    labels = jnp.arange(prompt_row.shape[0], dtype=jnp.int32)
    prompt_tok = lax.optimization_barrier(jnp.sum(jnp.where(segment_row[:, None] == labels[None, :], prompt_row[None, :], 0), axis=1))
    live_mask = earlier >= prompt_tok
    live_count = jnp.sum(live_mask.astype(jnp.int32))
    return (allowed, live_mask, live_count)

def replica_update(operands):
    token_block, query_block, key_block, teacher_block, segment_row, prompt_row, weight, moment = operands
    tok_count = token_block.shape[0]
    heads_here = weight.shape[1] // HEAD_DIM
    values = jnp.dot(token_block, weight, preferred_element_type=jnp.float32).astype(jnp.bfloat16)
    values = lax.optimization_barrier(values)
    query_split = query_block.reshape(tok_count, heads_here, HEAD_DIM).astype(jnp.float32)
    key_split = key_block.reshape(tok_count, heads_here, HEAD_DIM).astype(jnp.float32)
    value_split = values.reshape(tok_count, heads_here, HEAD_DIM).astype(jnp.float32)
    allowed, live_mask, live_count = loss_layout(segment_row, prompt_row)
    scores = jnp.einsum('thd,uhd->htu', query_split, key_split) / math.sqrt(HEAD_DIM)
    scores = jnp.where(allowed[None], scores, -jnp.inf)
    attention = jax.nn.softmax(scores, axis=-1).astype(jnp.bfloat16)
    attention = lax.optimization_barrier(attention)
    attended = jnp.einsum('htu,uhd->thd', attention.astype(jnp.float32), value_split)
    residue = attended - teacher_block.reshape(tok_count, heads_here, HEAD_DIM).astype(jnp.float32)
    errors = (jnp.where(live_mask[:, None, None], residue, 0.0) / live_count.astype(jnp.float32)).astype(jnp.bfloat16)
    errors = lax.optimization_barrier(errors)
    dvalues = jnp.einsum('htu,thd->uhd', attention.astype(jnp.float32), errors.astype(jnp.float32)).astype(jnp.bfloat16)
    dvalues = dvalues.reshape(tok_count, heads_here * HEAD_DIM)
    gradient = jnp.dot(token_block.T, dvalues, preferred_element_type=jnp.float32)
    moment_new = (MOMENTUM_DECAY * moment.astype(jnp.float32) + gradient).astype(jnp.bfloat16)
    moment_new = lax.optimization_barrier(moment_new)
    stepped = (weight.astype(jnp.float32) - LEARN_RATE * moment_new.astype(jnp.float32)).astype(jnp.bfloat16)
    return (moment_new, stepped)

def reference(hidden_rows, query_heads, key_heads, teacher_out, segment_ids, prompt_lens, gossip_step, value_weight, momentum):
    levels = N_REP.bit_length() - 1
    replica_ids = jnp.arange(N_REP, dtype=jnp.int32)
    weight_now = value_weight
    moment = momentum
    for step_index in range(STEPS):
        moment, stepped = lax.map(replica_update, (hidden_rows[:, step_index], query_heads[:, step_index], key_heads[:, step_index], teacher_out[:, step_index], segment_ids[:, step_index], prompt_lens[:, step_index], weight_now, moment))
        stepped = lax.optimization_barrier(stepped)
        bit_now = ((gossip_step[0] + step_index) % levels).astype(jnp.int32)
        partner_ids = jnp.bitwise_xor(replica_ids, jnp.left_shift(jnp.int32(1), bit_now))
        partner = jnp.take(stepped, partner_ids, axis=0)
        weight_now = ((stepped.astype(jnp.float32) + partner.astype(jnp.float32)) * 0.5).astype(jnp.bfloat16)
    return (weight_now, moment)
```

```python
import functools
import math

import jax
import jax.numpy as jnp
from jax import lax
from jax.experimental import pallas as pl
from jax.experimental.pallas import tpu as pltpu
from jax.sharding import PartitionSpec as P

HEAD_DIM = 128
LEARN_RATE = 0.1
MOMENTUM_DECAY = 0.9
LEVELS = 6
TOK = 256
ROWS = 2048
COLS = 256
TP = 8
SHARD = TOK // TP
HALF = SHARD // 2
CHUNKS = 8
CROWS = ROWS // CHUNKS
F32 = jnp.float32
BF16 = jnp.bfloat16
MESH = pl.DeviceIdType.MESH


def remote(src, dst, send, recv, device):
    return pltpu.make_async_remote_copy(
        src_ref=src, dst_ref=dst, send_sem=send, recv_sem=recv, device_id=device, device_id_type=MESH
    )


def partner_of(rep, bit):
    size = 1 << bit
    return rep + size * (1 - 2 * ((rep // size) % 2))


def kernel(
    bit_a, bit_b,
    hid, qry, key, tea, seg, prm, wgt, mom,
    w_out, m_out,
    x, qv, kv, tv, segv, prmv, wv, mv, stepped, landed, att, att_t, live, vals,
    load_sem, x_send, x_recv, g_send, g_recv, out_sem,
):
    rep = lax.axis_index("rep")
    tp = lax.axis_index("tp")
    row = (tp // 4) * 4
    right = row + (tp + 1) % 4
    left = row + (tp + 3) % 4
    cross = (tp + 4) % 8
    cross_right = (right + 4) % 8
    cross_left = (left + 4) % 8
    to_right = (rep, right)
    to_left = (rep, left)
    to_cross = (rep, cross)
    peers = ((partner_of(rep, bit_a), tp), (partner_of(rep, bit_b), tp))

    own_load = [pltpu.make_async_copy(hid.at[0, s], x.at[s, tp], load_sem.at[s]) for s in range(2)]
    loads = [
        pltpu.make_async_copy(seg.at[0], segv, load_sem.at[2]),
        pltpu.make_async_copy(prm.at[0], prmv, load_sem.at[3]),
        pltpu.make_async_copy(qry.at[0], qv, load_sem.at[4]),
        pltpu.make_async_copy(key.at[0], kv, load_sem.at[5]),
        pltpu.make_async_copy(tea.at[0], tv, load_sem.at[6]),
        pltpu.make_async_copy(wgt.at[0], wv, load_sem.at[7]),
        pltpu.make_async_copy(mom.at[0], mv, load_sem.at[8]),
    ]
    for copy in own_load + loads:
        copy.start()

    barrier = pltpu.get_barrier_semaphore()
    for device in (to_right, to_left, to_cross) + peers:
        pl.semaphore_signal(barrier, inc=1, device_id=device, device_id_type=MESH)
    pl.semaphore_wait(barrier, 5)

    route = (
        (tp, to_right, None),
        (tp, to_left, None),
        (tp, to_cross, None),
        (left, to_right, 0),
        (right, to_left, 1),
        (cross, to_right, None),
        (cross, to_left, None),
        (cross_left, to_right, 0),
        (cross_right, to_left, 1),
    )

    def hop(s, n):
        slot, device, half = route[n]
        part = x.at[s, slot] if half is None else x.at[s, slot, pl.ds(half * HALF, HALF)]
        return remote(part, part, x_send.at[s, n], x_recv.at[s, n], device)

    def stage_a(s):
        own_load[s].wait()
        for n in (2, 0, 1):
            hop(s, n).start()

    def stage_b(s):
        for arrived, onward in ((0, (3,)), (1, (4,)), (2, (5, 6))):
            hop(s, arrived).wait_recv()
            for n in onward:
                hop(s, n).start()

    def stage_c(s):
        for arrived, onward in ((5, 7), (6, 8)):
            hop(s, arrived).wait_recv()
            hop(s, onward).start()

    def stage_d(s):
        for n in (3, 4, 7, 8):
            hop(s, n).wait_recv()

    def stage_end(s):
        for n in range(9):
            hop(s, n).wait_send()

    def attention(s):
        ids = jnp.broadcast_to(segv[pl.ds(s, 1), :].astype(F32), (TOK, TOK))
        ids_t = ids.T
        rows = lax.broadcasted_iota(jnp.int32, (TOK, TOK), 0)
        columns = lax.broadcasted_iota(jnp.int32, (TOK, TOK), 1)
        same = ids == ids_t
        allowed = same & (columns <= rows)
        place = jnp.sum(jnp.where(same & (columns < rows), 1.0, 0.0), axis=1, keepdims=True)
        lens = jnp.broadcast_to(prmv[pl.ds(s, 1), :].astype(F32), (TOK, 8))
        labels = lax.broadcasted_iota(jnp.int32, (TOK, 8), 1).astype(F32)
        prompt = jnp.sum(jnp.where(ids_t[:, :8] == labels, lens, 0.0), axis=1, keepdims=True)
        alive = jnp.where(place >= prompt, 1.0, 0.0)
        count = jnp.sum(alive, axis=0, keepdims=True)
        live[s] = jnp.broadcast_to(alive / count, (TOK, 128))
        for h in range(2):
            cut = pl.ds(h * HEAD_DIM, HEAD_DIM)
            scores = lax.dot_general(
                qv[s, :, cut], kv[s, :, cut], (((1,), (1,)), ((), ())), preferred_element_type=F32
            ) / math.sqrt(HEAD_DIM)
            scores = jnp.where(allowed, scores, -jnp.inf)
            top = jnp.max(scores, axis=1, keepdims=True)
            weights = jnp.exp(scores - top)
            soft = weights / jnp.sum(weights, axis=1, keepdims=True)
            att[s, h] = soft.astype(BF16)
            att_t[s, h] = soft.T.astype(BF16)

    def value_grad(s, values):
        parts = []
        for h in range(2):
            cut = slice(h * HEAD_DIM, (h + 1) * HEAD_DIM)
            attended = jnp.dot(att[s, h], values[:, cut], preferred_element_type=F32)
            residue = attended - tv[s, :, cut].astype(F32)
            errors = (residue * live[s]).astype(BF16)
            parts.append(jnp.dot(att_t[s, h], errors, preferred_element_type=F32).astype(BF16))
        return jnp.concatenate(parts, axis=1)

    def send(s, i):
        cut = pl.ds(i * CROWS, CROWS)
        return remote(
            stepped.at[s, cut], landed.at[s, cut], g_send.at[s, i], g_recv.at[s, i], peers[s]
        )

    def out_copy(n, i):
        cut = pl.ds(i * CROWS, CROWS)
        source, target = ((wv, w_out), (mv, m_out))[n]
        return pltpu.make_async_copy(source.at[cut], target.at[0, cut], out_sem.at[n, i])

    def update(s, dvalues):
        vals[...] = dvalues

        def body(i, carry):
            cut = pl.ds(pl.multiple_of(i * CROWS, CROWS), CROWS)
            lhs = x[s, :, :, cut].reshape(TOK, CROWS)
            grad = lax.dot_general(
                lhs, vals[...], (((0,), (0,)), ((), ())), preferred_element_type=F32
            )
            moment = (MOMENTUM_DECAY * mv[cut, :].astype(F32) + grad).astype(BF16)
            mv[cut, :] = moment
            stepped[s, cut, :] = (
                wv[cut, :].astype(F32) - LEARN_RATE * moment.astype(F32)
            ).astype(BF16)
            send(s, i).start()
            if s == 1:
                out_copy(1, i).start()
            return carry

        lax.fori_loop(0, CHUNKS, body, 0)

    def average(s, i):
        cut = pl.ds(pl.multiple_of(i * CROWS, CROWS), CROWS)
        send(s, i).wait_recv()
        mean = (stepped[s, cut, :].astype(F32) + landed[s, cut, :].astype(F32)) * 0.5
        wv[cut, :] = mean.astype(BF16)

    stage_a(0)
    for copy in loads[:5]:
        copy.wait()
    attention(0)
    stage_b(0)
    attention(1)
    stage_c(0)
    stage_a(1)
    for copy in loads[5:]:
        copy.wait()
    stage_d(0)

    values = jnp.dot(
        x[0].reshape(TOK, ROWS), wv[...], preferred_element_type=F32
    ).astype(BF16)
    dvalues = value_grad(0, values)
    stage_b(1)
    update(0, dvalues)
    stage_c(1)
    stage_d(1)

    def first_gossip(i, total):
        average(0, i)
        cut = pl.ds(pl.multiple_of(i * CROWS, CROWS), CROWS)
        return total + jnp.dot(
            x[1, :, :, cut].reshape(TOK, CROWS), wv[cut, :], preferred_element_type=F32
        )

    values = lax.fori_loop(0, CHUNKS, first_gossip, jnp.zeros((TOK, COLS), F32)).astype(BF16)
    update(1, value_grad(1, values))

    def second_gossip(i, carry):
        average(1, i)
        out_copy(0, i).start()
        return carry

    lax.fori_loop(0, CHUNKS, second_gossip, 0)

    def finish(i, carry):
        for s in range(2):
            send(s, i).wait_send()
            out_copy(s, i).wait()
        return carry

    lax.fori_loop(0, CHUNKS, finish, 0)
    stage_end(0)
    stage_end(1)


def fused(bit, *operands):
    hid, qry, key, tea, seg, prm, wgt, mom = operands
    any_space = pl.BlockSpec(memory_space=pl.ANY)
    dma = pltpu.SemaphoreType.DMA
    return pl.pallas_call(
        functools.partial(kernel, bit, (bit + 1) % LEVELS),
        out_shape=(
            jax.ShapeDtypeStruct(wgt.shape, BF16),
            jax.ShapeDtypeStruct(mom.shape, BF16),
        ),
        in_specs=[any_space] * 8,
        out_specs=(any_space, any_space),
        scratch_shapes=[
            pltpu.VMEM((2, TP, SHARD, ROWS), BF16),
            pltpu.VMEM((2, TOK, COLS), BF16),
            pltpu.VMEM((2, TOK, COLS), BF16),
            pltpu.VMEM((2, TOK, COLS), BF16),
            pltpu.VMEM((2, TOK), jnp.int32),
            pltpu.VMEM((2, 8), jnp.int32),
            pltpu.VMEM((ROWS, COLS), BF16),
            pltpu.VMEM((ROWS, COLS), BF16),
            pltpu.VMEM((2, ROWS, COLS), BF16),
            pltpu.VMEM((2, ROWS, COLS), BF16),
            pltpu.VMEM((2, 2, TOK, TOK), BF16),
            pltpu.VMEM((2, 2, TOK, TOK), BF16),
            pltpu.VMEM((2, TOK, 128), F32),
            pltpu.VMEM((TOK, COLS), BF16),
            dma((9,)),
            dma((2, 9)),
            dma((2, 9)),
            dma((2, CHUNKS)),
            dma((2, CHUNKS)),
            dma((2, CHUNKS)),
        ],
        compiler_params=pltpu.CompilerParams(
            collective_id=bit, has_side_effects=True, vmem_limit_bytes=56 * 1024 * 1024
        ),
        name=f"gossip_{bit}",
    )(*operands)


def per_device(hid, qry, key, tea, seg, prm, gossip_step, wgt, mom):
    bit = gossip_step[0] % LEVELS
    branches = [functools.partial(fused, level) for level in range(LEVELS)]
    return lax.switch(bit, branches, hid, qry, key, tea, seg, prm, wgt, mom)


def solution(mesh):
    in_specs = (
        P("rep", None, "tp", None),
        P("rep", None, None, "tp"),
        P("rep", None, None, "tp"),
        P("rep", None, None, "tp"),
        P("rep", None, None),
        P("rep", None, None),
        P(),
        P("rep", None, "tp"),
        P("rep", None, "tp"),
    )
    out_specs = (P("rep", None, "tp"), P("rep", None, "tp"))
    return jax.shard_map(
        per_device, mesh=mesh, in_specs=in_specs, out_specs=out_specs, check_vma=False
    )
```

```python
import functools
import math

import jax
import jax.numpy as jnp
from jax import lax
from jax.experimental import pallas as pl
from jax.experimental.pallas import tpu as pltpu
from jax.sharding import PartitionSpec as P

HEAD_DIM = 128
LEARN_RATE = 0.1
MOMENTUM_DECAY = 0.9
LEVELS = 6
TOK = 256
ROWS = 2048
COLS = 256
TP = 8
SHARD = TOK // TP
HALF = ROWS // 2
CHUNKS = 8
CROWS = ROWS // CHUNKS
F32 = jnp.float32
BF16 = jnp.bfloat16
MESH = pl.DeviceIdType.MESH


def remote(src, dst, send, recv, device):
    return pltpu.make_async_remote_copy(
        src_ref=src, dst_ref=dst, send_sem=send, recv_sem=recv, device_id=device, device_id_type=MESH
    )


def partner_of(rep, bit):
    size = 1 << bit
    return rep + size * (1 - 2 * ((rep // size) % 2))


def kernel(
    bit_a, bit_b,
    hid, qry, key, tea, seg, prm, wgt, mom,
    w_out, m_out,
    x, qv, kv, tv, segv, prmv, wv, mv, stepped, landed, held, att, att_t, live, dvals, total,
    load_sem, x_send, x_recv, g_send, g_recv, low_send, low_recv, out_sem,
):
    early = bit_a <= 2
    lean = bit_a <= 1
    rep = lax.axis_index("rep")
    tp = lax.axis_index("tp")
    row = (tp // 4) * 4
    right = row + (tp + 1) % 4
    left = row + (tp + 3) % 4
    cross = (tp + 4) % 8
    far = row + (tp + 2) % 4
    cross_right = (right + 4) % 8
    cross_left = (left + 4) % 8
    to_right = (rep, right)
    to_left = (rep, left)
    to_cross = (rep, cross)
    peers = ((partner_of(rep, bit_a), tp), (partner_of(rep, bit_b), tp))

    own_load = [pltpu.make_async_copy(hid.at[0, s], x.at[s, tp], load_sem.at[s]) for s in range(2)]
    loads = [
        pltpu.make_async_copy(seg.at[0], segv, load_sem.at[2]),
        pltpu.make_async_copy(prm.at[0], prmv, load_sem.at[3]),
        pltpu.make_async_copy(qry.at[0], qv, load_sem.at[4]),
        pltpu.make_async_copy(key.at[0], kv, load_sem.at[5]),
        pltpu.make_async_copy(tea.at[0], tv, load_sem.at[6]),
        pltpu.make_async_copy(wgt.at[0], wv, load_sem.at[7]),
        pltpu.make_async_copy(mom.at[0], mv, load_sem.at[8]),
    ]
    for copy in own_load + loads:
        copy.start()

    barrier = pltpu.get_barrier_semaphore()
    for device in (to_right, to_left, to_cross) + peers:
        pl.semaphore_signal(barrier, inc=1, device_id=device, device_id_type=MESH)
    pl.semaphore_wait(barrier, 5)

    route = (
        (tp, to_right, 0),
        (tp, to_left, 1),
        (tp, to_cross, 0),
        (tp, to_cross, 1),
        (tp, to_right, 1),
        (tp, to_left, 0),
        (left, to_right, 0),
        (right, to_left, 1),
        (cross, to_right, 0),
        (cross, to_left, 0),
        (cross, to_right, 1),
        (cross, to_left, 1),
        (far, to_cross, 0),
        (far, to_cross, 1),
    )

    lean_route = route[:12] + ((cross_left, to_right, 0), (cross_right, to_left, 1))

    def hop(s, n):
        slot, device, half = (lean_route if lean and s else route)[n]
        part = x.at[s, slot, :, pl.ds(half * HALF, HALF)]
        return remote(part, part, x_send.at[s, n], x_recv.at[s, n], device)

    def start(s, *hops):
        for n in hops:
            hop(s, n).start()

    def stage_a(s):
        start(s, 2, 0, 1, 3, 4, 5)

    def stage_b(s):
        for arrived, onward in ((0, (6,)), (1, (7,)), (2, (8, 9)), (3, (10, 11))):
            hop(s, arrived).wait_recv()
            start(s, *onward)

    def stage_c(s):
        for arrived, onward in ((8, 12), (11, 13)) if lean and s else ((6, 12), (7, 13)):
            hop(s, arrived).wait_recv()
            start(s, onward)

    def stage_d(s):
        for n in (4, 5, 6, 7, 9, 10, 12, 13) if lean and s else (4, 5, 8, 9, 10, 11, 12, 13):
            hop(s, n).wait_recv()

    def stage_end(s):
        for n in range(14):
            hop(s, n).wait_send()

    def attention(s):
        ids = jnp.broadcast_to(segv[pl.ds(s, 1), :].astype(F32), (TOK, TOK))
        ids_t = ids.T
        rows = lax.broadcasted_iota(jnp.int32, (TOK, TOK), 0)
        columns = lax.broadcasted_iota(jnp.int32, (TOK, TOK), 1)
        same = ids == ids_t
        allowed = same & (columns <= rows)
        place = jnp.sum(jnp.where(same & (columns < rows), 1.0, 0.0), axis=1, keepdims=True)
        lens = jnp.broadcast_to(prmv[pl.ds(s, 1), :].astype(F32), (TOK, 8))
        labels = lax.broadcasted_iota(jnp.int32, (TOK, 8), 1).astype(F32)
        prompt = jnp.sum(jnp.where(ids_t[:, :8] == labels, lens, 0.0), axis=1, keepdims=True)
        alive = jnp.where(place >= prompt, 1.0, 0.0)
        count = jnp.sum(alive, axis=0, keepdims=True)
        live[s] = jnp.broadcast_to(alive / count, (TOK, 128))
        for h in range(2):
            cut = pl.ds(h * HEAD_DIM, HEAD_DIM)
            scores = lax.dot_general(
                qv[s, :, cut], kv[s, :, cut], (((1,), (1,)), ((), ())), preferred_element_type=F32
            ) / math.sqrt(HEAD_DIM)
            scores = jnp.where(allowed, scores, -jnp.inf)
            top = jnp.max(scores, axis=1, keepdims=True)
            weights = jnp.exp(scores - top)
            soft = weights / jnp.sum(weights, axis=1, keepdims=True)
            att[s, h] = soft.astype(BF16)
            att_t[s, h] = soft.T.astype(BF16)

    def value_grad(s, values):
        parts = []
        for h in range(2):
            cut = slice(h * HEAD_DIM, (h + 1) * HEAD_DIM)
            attended = jnp.dot(att[s, h], values[:, cut], preferred_element_type=F32)
            residue = attended - tv[s, :, cut].astype(F32)
            errors = (residue * live[s]).astype(BF16)
            parts.append(jnp.dot(att_t[s, h], errors, preferred_element_type=F32).astype(BF16))
        return jnp.concatenate(parts, axis=1)

    def send(s, i):
        cut = pl.ds(i * CROWS, CROWS)
        return remote(
            stepped.at[s, cut], landed.at[s, cut], g_send.at[s, i], g_recv.at[s, i], peers[s]
        )

    def out_copy(n, i):
        cut = pl.ds(i * CROWS, CROWS)
        source, target = ((wv, w_out), (mv, m_out))[n]
        return pltpu.make_async_copy(source.at[cut], target.at[0, cut], out_sem.at[n, i])

    def rows_of(i):
        return pl.ds(pl.multiple_of(i * CROWS, CROWS), CROWS)

    def grad_rows(n, i, dvalues):
        lhs = x[n, :, :, rows_of(i)].reshape(TOK, CROWS)
        return lax.dot_general(lhs, dvalues, (((0,), (0,)), ((), ())), preferred_element_type=F32)

    def update(s, i, target):
        cut = rows_of(i)
        moment = (
            MOMENTUM_DECAY * mv[cut, :].astype(F32) + grad_rows(s, i, dvals[s])
        ).astype(BF16)
        mv[cut, :] = moment
        target[cut, :] = (wv[cut, :].astype(F32) - LEARN_RATE * moment.astype(F32)).astype(BF16)

    def average(s, i):
        cut = rows_of(i)
        send(s, i).wait_recv()
        mean = (stepped[s, cut, :].astype(F32) + landed[s, cut, :].astype(F32)) * 0.5
        wv[cut, :] = mean.astype(BF16)

    def add_values(i, count=1):
        cut = pl.ds(pl.multiple_of(i * CROWS, CROWS), count * CROWS)
        total[...] += jnp.dot(
            x[1, :, :, cut].reshape(TOK, count * CROWS), wv[cut, :], preferred_element_type=F32
        )

    def loop(first, last, body):
        def step(i, carry):
            body(i)
            return carry

        lax.fori_loop(first, last, step, 0)

    def first_update(i):
        update(0, i, stepped.at[0])
        send(0, i).start()

    def first_gossip(i):
        average(0, i)
        if early:
            cut = rows_of(i)
            ahead = wv[cut, :].astype(F32) - (LEARN_RATE * MOMENTUM_DECAY) * mv[cut, :].astype(F32)
            stepped[1, cut, :] = ahead.astype(BF16)
            send(1, i).start()

    def first_gossip_values(i):
        first_gossip(i)
        add_values(i)

    def second_update(i):
        if early:
            update(1, i, held)
        else:
            update(1, i, stepped.at[1])
            send(1, i).start()
        out_copy(1, i).start()

    def second_gossip(i):
        if early:
            cut = rows_of(i)
            send(1, i).wait_recv()
            theirs = landed[1, cut, :].astype(F32) - LEARN_RATE * grad_rows(2, i, dvals[2])
            wv[cut, :] = ((held[cut, :].astype(F32) + theirs) * 0.5).astype(BF16)
        else:
            average(1, i)
        out_copy(0, i).start()

    def finish(i):
        for s in range(2):
            send(s, i).wait_send()
            out_copy(s, i).wait()

    if early:
        their_rows = remote(
            hid.at[0, 1], x.at[2, tp], low_send.at[0], low_recv.at[0], peers[1]
        )
        their_grad = remote(dvals.at[1], dvals.at[2], low_send.at[1], low_recv.at[1], peers[1])

    own_load[0].wait()
    stage_a(0)
    if early and bit_b > 1:
        their_rows.start()
    for copy in loads[:5]:
        copy.wait()
    attention(0)
    stage_b(0)
    stage_c(0)
    own_load[1].wait()
    if lean:
        start(1, 2, 3)
        if bit_b == 1:
            their_rows.start()
    attention(1)
    for copy in loads[5:]:
        copy.wait()
    stage_d(0)
    if lean:
        start(1, 0, 1, 4, 5)
        their_rows.wait_recv()
        start(2, 2, 3)
    else:
        stage_a(1)

    values = jnp.dot(
        x[0].reshape(TOK, ROWS), wv[...], preferred_element_type=F32
    ).astype(BF16)
    dvals[0] = value_grad(0, values)
    loop(0, CHUNKS, first_update)
    total[...] = jnp.zeros((TOK, COLS), F32)
    stage_b(1)
    if bit_a == 0:
        loop(0, CHUNKS, first_gossip)
        stage_c(1)
        stage_d(1)
        start(2, 0, 1, 4, 5)
        add_values(0, CHUNKS)
    else:
        stage_c(1)
        if lean:
            start(2, 0, 1, 4, 5)
        elif early:
            their_rows.wait_recv()
            stage_a(2)
        loop(0, 4, first_gossip)
        stage_d(1)
        add_values(0, 4)
        if early:
            stage_b(2)
        loop(4, 6, first_gossip_values)
        if early:
            stage_c(2)
        loop(6, CHUNKS, first_gossip_values)

    dvals[1] = value_grad(1, total[...].astype(BF16))
    if early:
        their_grad.start()
    if bit_a == 0:
        stage_b(2)
    loop(0, CHUNKS, second_update)
    if early:
        if bit_a == 0:
            stage_c(2)
        stage_d(2)
        their_grad.wait_recv()
    loop(0, CHUNKS, second_gossip)
    loop(0, CHUNKS, finish)
    stage_end(0)
    stage_end(1)
    if early:
        stage_end(2)
        their_rows.wait_send()
        their_grad.wait_send()


def fused(bit, *operands):
    hid, qry, key, tea, seg, prm, wgt, mom = operands
    any_space = pl.BlockSpec(memory_space=pl.ANY)
    dma = pltpu.SemaphoreType.DMA
    return pl.pallas_call(
        functools.partial(kernel, bit, (bit + 1) % LEVELS),
        out_shape=(
            jax.ShapeDtypeStruct(wgt.shape, BF16),
            jax.ShapeDtypeStruct(mom.shape, BF16),
        ),
        in_specs=[any_space] * 8,
        out_specs=(any_space, any_space),
        scratch_shapes=[
            pltpu.VMEM((3, TP, SHARD, ROWS), BF16),
            pltpu.VMEM((2, TOK, COLS), BF16),
            pltpu.VMEM((2, TOK, COLS), BF16),
            pltpu.VMEM((2, TOK, COLS), BF16),
            pltpu.VMEM((2, TOK), jnp.int32),
            pltpu.VMEM((2, 8), jnp.int32),
            pltpu.VMEM((ROWS, COLS), BF16),
            pltpu.VMEM((ROWS, COLS), BF16),
            pltpu.VMEM((2, ROWS, COLS), BF16),
            pltpu.VMEM((2, ROWS, COLS), BF16),
            pltpu.VMEM((ROWS, COLS), BF16),
            pltpu.VMEM((2, 2, TOK, TOK), BF16),
            pltpu.VMEM((2, 2, TOK, TOK), BF16),
            pltpu.VMEM((2, TOK, 128), F32),
            pltpu.VMEM((3, TOK, COLS), BF16),
            pltpu.VMEM((TOK, COLS), F32),
            dma((9,)),
            dma((3, 14)),
            dma((3, 14)),
            dma((2, CHUNKS)),
            dma((2, CHUNKS)),
            dma((2,)),
            dma((2,)),
            dma((2, CHUNKS)),
        ],
        compiler_params=pltpu.CompilerParams(
            collective_id=bit, has_side_effects=True, vmem_limit_bytes=56 * 1024 * 1024
        ),
        name=f"gossip_{bit}",
    )(*operands)


def per_device(hid, qry, key, tea, seg, prm, gossip_step, wgt, mom):
    bit = gossip_step[0] % LEVELS
    branches = [functools.partial(fused, level) for level in range(LEVELS)]
    return lax.switch(bit, branches, hid, qry, key, tea, seg, prm, wgt, mom)


def solution(mesh):
    in_specs = (
        P("rep", None, "tp", None),
        P("rep", None, None, "tp"),
        P("rep", None, None, "tp"),
        P("rep", None, None, "tp"),
        P("rep", None, None),
        P("rep", None, None),
        P(),
        P("rep", None, "tp"),
        P("rep", None, "tp"),
    )
    out_specs = (P("rep", None, "tp"), P("rep", None, "tp"))
    return jax.shard_map(
        per_device, mesh=mesh, in_specs=in_specs, out_specs=out_specs, check_vma=False
    )
```

```python
import functools
import math

import jax
import jax.numpy as jnp
from jax import lax
from jax.experimental import pallas as pl
from jax.experimental.pallas import tpu as pltpu
from jax.sharding import PartitionSpec as P

HEAD_DIM = 128
LEARN_RATE = 0.1
MOMENTUM_DECAY = 0.9
LEVELS = 6
TOK = 256
ROWS = 2048
COLS = 256
TP = 8
SHARD = TOK // TP
HALF = ROWS // 2
CHUNKS = 8
CROWS = ROWS // CHUNKS
F32 = jnp.float32
BF16 = jnp.bfloat16
MESH = pl.DeviceIdType.MESH


def remote(src, dst, send, recv, device):
    return pltpu.make_async_remote_copy(
        src_ref=src, dst_ref=dst, send_sem=send, recv_sem=recv, device_id=device, device_id_type=MESH
    )


def partner_of(rep, bit):
    size = 1 << bit
    return rep + size * (1 - 2 * ((rep // size) % 2))


def kernel(
    bit_a, bit_b,
    hid, qry, key, tea, seg, prm, wgt, mom,
    w_out, m_out,
    x, qv, kv, tv, segv, prmv, wv, mv, stepped, landed, held, att, att_t, live, vals, dvals, total,
    load_sem, x_send, x_recv, g_send, g_recv, low_send, low_recv, out_sem,
):
    early = bit_a in (1, 2)
    paired = bit_b == 0
    lean = bit_a == 1
    rep = lax.axis_index("rep")
    tp = lax.axis_index("tp")
    row = (tp // 4) * 4
    right = row + (tp + 1) % 4
    left = row + (tp + 3) % 4
    cross = (tp + 4) % 8
    far = row + (tp + 2) % 4
    cross_right = (right + 4) % 8
    cross_left = (left + 4) % 8
    to_right = (rep, right)
    to_left = (rep, left)
    to_cross = (rep, cross)
    peers = ((partner_of(rep, bit_a), tp), (partner_of(rep, bit_b), tp))

    own_load = [pltpu.make_async_copy(hid.at[0, s], x.at[s, tp], load_sem.at[s]) for s in range(2)]
    loads = [
        pltpu.make_async_copy(seg.at[0], segv, load_sem.at[2]),
        pltpu.make_async_copy(prm.at[0], prmv, load_sem.at[3]),
        pltpu.make_async_copy(qry.at[0], qv, load_sem.at[4]),
        pltpu.make_async_copy(key.at[0], kv, load_sem.at[5]),
        pltpu.make_async_copy(tea.at[0], tv, load_sem.at[6]),
        pltpu.make_async_copy(wgt.at[0], wv, load_sem.at[7]),
        pltpu.make_async_copy(mom.at[0], mv, load_sem.at[8]),
    ]
    for copy in own_load + loads:
        copy.start()

    barrier = pltpu.get_barrier_semaphore()
    for device in (to_right, to_left, to_cross) + peers:
        pl.semaphore_signal(barrier, inc=1, device_id=device, device_id_type=MESH)
    pl.semaphore_wait(barrier, 5)

    route = (
        (tp, to_right, 0),
        (tp, to_left, 1),
        (tp, to_cross, 0),
        (tp, to_cross, 1),
        (tp, to_right, 1),
        (tp, to_left, 0),
        (left, to_right, 0),
        (right, to_left, 1),
        (cross, to_right, 0),
        (cross, to_left, 0),
        (cross, to_right, 1),
        (cross, to_left, 1),
        (far, to_cross, 0),
        (far, to_cross, 1),
    )

    lean_route = route[:12] + ((cross_left, to_right, 0), (cross_right, to_left, 1))

    def hop(s, n):
        slot, device, half = (lean_route if lean and s else route)[n]
        part = x.at[s, slot, :, pl.ds(half * HALF, HALF)]
        return remote(part, part, x_send.at[s, n], x_recv.at[s, n], device)

    def start(s, *hops):
        for n in hops:
            hop(s, n).start()

    def stage_a(s):
        start(s, 2, 0, 1, 3, 4, 5)

    def stage_b(s):
        for arrived, onward in ((0, (6,)), (1, (7,)), (2, (8, 9)), (3, (10, 11))):
            hop(s, arrived).wait_recv()
            start(s, *onward)

    def stage_c(s):
        for arrived, onward in ((8, 12), (11, 13)) if lean and s else ((6, 12), (7, 13)):
            hop(s, arrived).wait_recv()
            start(s, onward)

    def stage_d(s):
        for n in (4, 5, 6, 7, 9, 10, 12, 13) if lean and s else (4, 5, 8, 9, 10, 11, 12, 13):
            hop(s, n).wait_recv()

    def stage_end(s):
        for n in range(14):
            hop(s, n).wait_send()

    def loop(first, last, body, unroll=False):
        def step(i, carry):
            body(i)
            return carry

        lax.fori_loop(first, last, step, 0, unroll=unroll)

    def attention(s):
        ids = jnp.broadcast_to(segv[pl.ds(s, 1), :].astype(F32), (TOK, TOK))
        ids_t = ids.T
        rows = lax.broadcasted_iota(jnp.int32, (TOK, TOK), 0)
        columns = lax.broadcasted_iota(jnp.int32, (TOK, TOK), 1)
        same = ids == ids_t
        allowed = same & (columns <= rows)
        place = jnp.sum(jnp.where(same & (columns < rows), 1.0, 0.0), axis=1, keepdims=True)
        lens = jnp.broadcast_to(prmv[pl.ds(s, 1), :].astype(F32), (TOK, 8))
        labels = lax.broadcasted_iota(jnp.int32, (TOK, 8), 1).astype(F32)
        prompt = jnp.sum(jnp.where(ids_t[:, :8] == labels, lens, 0.0), axis=1, keepdims=True)
        alive = jnp.where(place >= prompt, 1.0, 0.0)
        count = jnp.sum(alive, axis=0, keepdims=True)
        live[s] = jnp.broadcast_to(alive / count, (TOK, 128))

        def one_head(h):
            cut = pl.ds(pl.multiple_of(h * HEAD_DIM, HEAD_DIM), HEAD_DIM)
            scores = lax.dot_general(
                qv[s, :, cut], kv[s, :, cut], (((1,), (1,)), ((), ())), preferred_element_type=F32
            ) / math.sqrt(HEAD_DIM)
            scores = jnp.where(allowed, scores, -jnp.inf)
            top = jnp.max(scores, axis=1, keepdims=True)
            weights = jnp.exp(scores - top)
            soft = weights / jnp.sum(weights, axis=1, keepdims=True)
            att[s, h] = soft.astype(BF16)
            att_t[s, h] = soft.T.astype(BF16)

        loop(0, 2, one_head)

    def value_grad(s, values):
        vals[...] = values

        def one_head(h):
            cut = pl.ds(pl.multiple_of(h * HEAD_DIM, HEAD_DIM), HEAD_DIM)
            attended = jnp.dot(att[s, h], vals[:, cut], preferred_element_type=F32)
            residue = attended - tv[s, :, cut].astype(F32)
            errors = (residue * live[s]).astype(BF16)
            dvals[s, :, cut] = jnp.dot(
                att_t[s, h], errors, preferred_element_type=F32
            ).astype(BF16)

        loop(0, 2, one_head)

    def rows_of(i):
        return pl.ds(pl.multiple_of(i * CROWS, CROWS), CROWS)

    def send(s, i):
        cut = pl.ds(i * CROWS, CROWS)
        return remote(
            stepped.at[s, cut], landed.at[s, cut], g_send.at[s, i], g_recv.at[s, i], peers[s]
        )

    def out_copy(n, i):
        cut = rows_of(i)
        source, target = ((wv, w_out), (mv, m_out))[n]
        return pltpu.make_async_copy(source.at[cut], target.at[0, cut], out_sem.at[n, i])

    def grad_rows(n, i, dvalues):
        lhs = x[n, :, :, rows_of(i)].reshape(TOK, CROWS)
        return lax.dot_general(lhs, dvalues, (((0,), (0,)), ((), ())), preferred_element_type=F32)

    def moment_rows(s, i):
        cut = rows_of(i)
        moment = (
            MOMENTUM_DECAY * mv[cut, :].astype(F32) + grad_rows(s, i, dvals[s])
        ).astype(BF16)
        mv[cut, :] = moment
        return moment

    def update(s, i, target):
        cut = rows_of(i)
        moment = moment_rows(s, i)
        target[cut, :] = (wv[cut, :].astype(F32) - LEARN_RATE * moment.astype(F32)).astype(BF16)

    def average(s, i):
        cut = rows_of(i)
        send(s, i).wait_recv()
        mean = (stepped[s, cut, :].astype(F32) + landed[s, cut, :].astype(F32)) * 0.5
        wv[cut, :] = mean.astype(BF16)

    def add_values(i, count=1):
        cut = pl.ds(pl.multiple_of(i * CROWS, CROWS), count * CROWS)
        total[...] += jnp.dot(
            x[1, :, :, cut].reshape(TOK, count * CROWS), wv[cut, :], preferred_element_type=F32
        )

    def first_update(i):
        update(0, i, stepped.at[0])
        send(0, i).start()

    def first_gossip(i):
        average(0, i)
        if early:
            cut = rows_of(i)
            ahead = wv[cut, :].astype(F32) - (LEARN_RATE * MOMENTUM_DECAY) * mv[cut, :].astype(F32)
            stepped[1, cut, :] = ahead.astype(BF16)
            send(1, i).start()

    def first_gossip_values(i):
        first_gossip(i)
        add_values(i)

    def second_update(i):
        if early:
            update(1, i, held)
        else:
            update(1, i, stepped.at[1])
            send(1, i).start()
        out_copy(1, i).start()

    def second_gossip(i):
        if early:
            cut = rows_of(i)
            send(1, i).wait_recv()
            theirs = landed[1, cut, :].astype(F32) - LEARN_RATE * grad_rows(2, i, dvals[2])
            wv[cut, :] = ((held[cut, :].astype(F32) + theirs) * 0.5).astype(BF16)
        else:
            average(1, i)
        out_copy(0, i).start()

    def finish(i):
        for s in range(2):
            send(s, i).wait_send()
            out_copy(s, i).wait()

    if early:
        their_rows = remote(
            hid.at[0, 1], x.at[2, tp], low_send.at[0], low_recv.at[0], peers[1]
        )
        their_grad = remote(dvals.at[1], dvals.at[2], low_send.at[1], low_recv.at[1], peers[1])
    if paired:
        their_rows = remote(
            hid.at[0, 1], x.at[2, tp], low_send.at[0], low_recv.at[0], peers[0]
        )
        product = remote(dvals.at[0], dvals.at[2], low_send.at[1], low_recv.at[1], peers[0])

    def paired_steps():
        quarter = CHUNKS // 2
        mine = (rep % 2) * quarter
        other = quarter - mine

        def crossing(n, k):
            base = (other, mine, other, mine)[n]
            cut = rows_of(base + k)
            source, target = (
                (stepped.at[0], landed.at[0]),
                (stepped.at[1], landed.at[1]),
                (mv, held),
                (wv, landed.at[0]),
            )[n]
            m = n // 2 * quarter + k
            return remote(
                source.at[cut],
                target.at[cut],
                g_send.at[n % 2, m],
                g_recv.at[n % 2, m],
                peers[1 - n] if n < 2 else peers[1],
            )

        def weight_out(k, theirs):
            cut = rows_of((other if theirs else mine) + k)
            source = landed.at[0] if theirs else wv
            sem = out_sem.at[0, k + quarter * theirs]
            return pltpu.make_async_copy(source.at[cut], w_out.at[0, cut], sem)

        def step_for_mate(k):
            update(0, other + k, stepped.at[0])
            crossing(0, k).start()

        def step_for_chip(k):
            update(0, mine + k, stepped.at[0])
            cut = rows_of(mine + k)
            crossing(0, k).wait_recv()
            both = (stepped[0, cut, :].astype(F32) + landed[0, cut, :].astype(F32)) * 0.5
            stepped[1, cut, :] = both.astype(BF16)
            crossing(1, k).start()

        def moment_for_mate(k):
            moment_rows(1, other + k)
            crossing(2, k).start()
            out_copy(1, other + k).start()

        def moment_for_chip(k):
            moment_rows(1, mine + k)
            out_copy(1, mine + k).start()

        def weights(k):
            cut = rows_of(mine + k)
            crossing(2, k).wait_recv()
            crossing(1, k).wait_recv()
            both = stepped[1, cut, :].astype(F32) + landed[1, cut, :].astype(F32)
            moments = mv[cut, :].astype(F32) + held[cut, :].astype(F32)
            wv[cut, :] = (both * 0.5 - (0.5 * LEARN_RATE) * moments).astype(BF16)
            crossing(3, k).start()
            weight_out(k, False).start()

        def weights_of_mate(k):
            crossing(3, k).wait_recv()
            weight_out(k, True).start()

        def end(k):
            for n in range(4):
                crossing(n, k).wait_send()
            weight_out(k, False).wait()
            weight_out(k, True).wait()
            out_copy(1, mine + k).wait()
            out_copy(1, other + k).wait()

        loop(0, quarter, step_for_mate)
        loop(0, quarter, step_for_chip)
        stage_b(1)
        stage_c(1)
        their_rows.wait_recv()
        stage_a(2)
        stage_d(1)
        total[...] = jnp.dot(
            x[1].reshape(TOK, ROWS), stepped[0], preferred_element_type=F32
        )
        stage_b(2)
        stage_c(2)
        stage_d(2)
        dvals[0] = jnp.dot(
            x[2].reshape(TOK, ROWS), stepped[0], preferred_element_type=F32
        ).astype(BF16)
        product.start()
        product.wait_recv()
        values = ((total[...] + dvals[2].astype(F32)) * 0.5).astype(BF16)
        value_grad(1, values)
        loop(0, quarter, moment_for_mate)
        loop(0, quarter, moment_for_chip)
        loop(0, quarter, weights)
        loop(0, quarter, weights_of_mate)
        loop(0, quarter, end)
        product.wait_send()
        their_rows.wait_send()
        for s in range(3):
            stage_end(s)

    own_load[0].wait()
    stage_a(0)
    if early or paired:
        their_rows.start()
    for copy in loads[:5]:
        copy.wait()
    attention(0)
    stage_b(0)
    stage_c(0)
    own_load[1].wait()
    if lean:
        start(1, 2, 3)
    elif bit_a == 0:
        stage_a(1)
    attention(1)
    for copy in loads[5:]:
        copy.wait()
    stage_d(0)
    if lean:
        start(1, 0, 1, 4, 5)
        their_rows.wait_recv()
        start(2, 2, 3)
    elif bit_a > 0:
        stage_a(1)

    values = jnp.dot(
        x[0].reshape(TOK, ROWS), wv[...], preferred_element_type=F32
    ).astype(BF16)
    value_grad(0, values)
    if paired:
        paired_steps()
        return
    if bit_a == 0:
        stage_b(1)
    loop(0, CHUNKS, first_update, bit_a == 0)
    total[...] = jnp.zeros((TOK, COLS), F32)
    if bit_a == 0:
        stage_c(1)
        loop(0, CHUNKS, first_gossip)
        stage_d(1)
        add_values(0, CHUNKS)
    else:
        stage_b(1)
        stage_c(1)
        if lean:
            start(2, 0, 1, 4, 5)
        elif early:
            their_rows.wait_recv()
            stage_a(2)
        loop(0, 4, first_gossip)
        stage_d(1)
        add_values(0, 4)
        if early:
            stage_b(2)
        loop(4, 6, first_gossip_values)
        if early:
            stage_c(2)
        loop(6, CHUNKS, first_gossip_values)

    value_grad(1, total[...].astype(BF16))
    if early:
        their_grad.start()
    loop(0, CHUNKS, second_update)
    if early:
        stage_d(2)
        their_grad.wait_recv()
    loop(0, CHUNKS, second_gossip, early)
    loop(0, CHUNKS, finish)
    stage_end(0)
    stage_end(1)
    if early:
        stage_end(2)
        their_rows.wait_send()
        their_grad.wait_send()


def fused(bit, *operands):
    hid, qry, key, tea, seg, prm, wgt, mom = operands
    any_space = pl.BlockSpec(memory_space=pl.ANY)
    dma = pltpu.SemaphoreType.DMA
    return pl.pallas_call(
        functools.partial(kernel, bit, (bit + 1) % LEVELS),
        out_shape=(
            jax.ShapeDtypeStruct(wgt.shape, BF16),
            jax.ShapeDtypeStruct(mom.shape, BF16),
        ),
        in_specs=[any_space] * 8,
        out_specs=(any_space, any_space),
        scratch_shapes=[
            pltpu.VMEM((3, TP, SHARD, ROWS), BF16),
            pltpu.VMEM((2, TOK, COLS), BF16),
            pltpu.VMEM((2, TOK, COLS), BF16),
            pltpu.VMEM((2, TOK, COLS), BF16),
            pltpu.VMEM((2, TOK), jnp.int32),
            pltpu.VMEM((2, 8), jnp.int32),
            pltpu.VMEM((ROWS, COLS), BF16),
            pltpu.VMEM((ROWS, COLS), BF16),
            pltpu.VMEM((2, ROWS, COLS), BF16),
            pltpu.VMEM((2, ROWS, COLS), BF16),
            pltpu.VMEM((ROWS, COLS), BF16),
            pltpu.VMEM((2, 2, TOK, TOK), BF16),
            pltpu.VMEM((2, 2, TOK, TOK), BF16),
            pltpu.VMEM((2, TOK, 128), F32),
            pltpu.VMEM((TOK, COLS), BF16),
            pltpu.VMEM((3, TOK, COLS), BF16),
            pltpu.VMEM((TOK, COLS), F32),
            dma((9,)),
            dma((3, 14)),
            dma((3, 14)),
            dma((2, CHUNKS)),
            dma((2, CHUNKS)),
            dma((2,)),
            dma((2,)),
            dma((2, CHUNKS)),
        ],
        compiler_params=pltpu.CompilerParams(
            collective_id=bit, has_side_effects=True, vmem_limit_bytes=56 * 1024 * 1024
        ),
        name=f"gossip_{bit}",
    )(*operands)


def per_device(hid, qry, key, tea, seg, prm, gossip_step, wgt, mom):
    bit = gossip_step[0] % LEVELS
    branches = [functools.partial(fused, level) for level in range(LEVELS)]
    return lax.switch(bit, branches, hid, qry, key, tea, seg, prm, wgt, mom)


def solution(mesh):
    in_specs = (
        P("rep", None, "tp", None),
        P("rep", None, None, "tp"),
        P("rep", None, None, "tp"),
        P("rep", None, None, "tp"),
        P("rep", None, None),
        P("rep", None, None),
        P(),
        P("rep", None, "tp"),
        P("rep", None, "tp"),
    )
    out_specs = (P("rep", None, "tp"), P("rep", None, "tp"))
    return jax.shard_map(
        per_device, mesh=mesh, in_specs=in_specs, out_specs=out_specs, check_vma=False
    )
```

```python
import functools
import math

import jax
import jax.numpy as jnp
from jax import lax
from jax.experimental import pallas as pl
from jax.experimental.pallas import tpu as pltpu
from jax.sharding import PartitionSpec as P

HEAD_DIM = 128
LEARN_RATE = 0.1
MOMENTUM_DECAY = 0.9
LEVELS = 6
REPS = 1 << LEVELS
TOK = 256
ROWS = 2048
COLS = 256
TP = 8
SHARD = TOK // TP
HALF = ROWS // 2
CHUNKS = 8
CROWS = ROWS // CHUNKS
F32 = jnp.float32
BF16 = jnp.bfloat16
MESH = pl.DeviceIdType.MESH


def remote(src, dst, send, recv, device):
    return pltpu.make_async_remote_copy(
        src_ref=src, dst_ref=dst, send_sem=send, recv_sem=recv, device_id=device, device_id_type=MESH
    )


def partner_of(rep, bit):
    size = 1 << bit
    return rep + size * (1 - 2 * ((rep // size) % 2))


def kernel(
    bit_a, bit_b,
    hid, qry, key, tea, seg, prm, wgt, mom,
    w_out, m_out,
    x, qv, kv, tv, segv, prmv, wv, mv, stepped, landed, held, att, att_t, live, vals, dvals, total,
    load_sem, x_send, x_recv, g_send, g_recv, low_send, low_recv, out_sem,
):
    early = bit_a in (1, 2)
    paired = bit_b == 0
    ring = bit_a == 4
    lean = bit_a == 1
    rep = lax.axis_index("rep")
    tp = lax.axis_index("tp")
    row = (tp // 4) * 4
    right = row + (tp + 1) % 4
    left = row + (tp + 3) % 4
    cross = (tp + 4) % 8
    far = row + (tp + 2) % 4
    cross_right = (right + 4) % 8
    cross_left = (left + 4) % 8
    to_right = (rep, right)
    to_left = (rep, left)
    to_cross = (rep, cross)
    partner = (partner_of(rep, bit_a), tp)
    peers = (partner, (partner_of(rep, bit_b), tp))
    if ring:
        peers = (((rep + (1 << bit_a)) % REPS, tp), ((rep + REPS - (1 << bit_a)) % REPS, tp))

    own_load = [pltpu.make_async_copy(hid.at[0, s], x.at[s, tp], load_sem.at[s]) for s in range(2)]
    loads = [
        pltpu.make_async_copy(seg.at[0], segv, load_sem.at[2]),
        pltpu.make_async_copy(prm.at[0], prmv, load_sem.at[3]),
        pltpu.make_async_copy(qry.at[0], qv, load_sem.at[4]),
        pltpu.make_async_copy(key.at[0], kv, load_sem.at[5]),
        pltpu.make_async_copy(tea.at[0], tv, load_sem.at[6]),
        pltpu.make_async_copy(wgt.at[0], wv, load_sem.at[7]),
        pltpu.make_async_copy(mom.at[0], mv, load_sem.at[8]),
    ]
    for copy in own_load + loads:
        copy.start()

    barrier = pltpu.get_barrier_semaphore()
    for device in (to_right, to_left, to_cross) + peers:
        pl.semaphore_signal(barrier, inc=1, device_id=device, device_id_type=MESH)
    pl.semaphore_wait(barrier, 5)

    route = (
        (tp, to_right, 0),
        (tp, to_left, 1),
        (tp, to_cross, 0),
        (tp, to_cross, 1),
        (tp, to_right, 1),
        (tp, to_left, 0),
        (left, to_right, 0),
        (right, to_left, 1),
        (cross, to_right, 0),
        (cross, to_left, 0),
        (cross, to_right, 1),
        (cross, to_left, 1),
        (far, to_cross, 0),
        (far, to_cross, 1),
    )

    lean_route = route[:12] + ((cross_left, to_right, 0), (cross_right, to_left, 1))

    def hop(s, n):
        slot, device, half = (lean_route if lean and s else route)[n]
        part = x.at[s, slot, :, pl.ds(half * HALF, HALF)]
        return remote(part, part, x_send.at[s, n], x_recv.at[s, n], device)

    def start(s, *hops):
        for n in hops:
            hop(s, n).start()

    def stage_a(s):
        start(s, 2, 0, 1, 3, 4, 5)

    def stage_b(s):
        for arrived, onward in ((0, (6,)), (1, (7,)), (2, (8, 9)), (3, (10, 11))):
            hop(s, arrived).wait_recv()
            start(s, *onward)

    def stage_c(s):
        for arrived, onward in ((8, 12), (11, 13)) if lean and s else ((6, 12), (7, 13)):
            hop(s, arrived).wait_recv()
            start(s, onward)

    def stage_d(s):
        for n in (4, 5, 6, 7, 9, 10, 12, 13) if lean and s else (4, 5, 8, 9, 10, 11, 12, 13):
            hop(s, n).wait_recv()

    def stage_end(s):
        for n in range(14):
            hop(s, n).wait_send()

    def loop(first, last, body):
        def step(i, carry):
            body(i)
            return carry

        lax.fori_loop(first, last, step, 0)

    def attention(s):
        ids = jnp.broadcast_to(segv[pl.ds(s, 1), :].astype(F32), (TOK, TOK))
        ids_t = ids.T
        rows = lax.broadcasted_iota(jnp.int32, (TOK, TOK), 0)
        columns = lax.broadcasted_iota(jnp.int32, (TOK, TOK), 1)
        same = ids == ids_t
        allowed = same & (columns <= rows)
        place = jnp.sum(jnp.where(same & (columns < rows), 1.0, 0.0), axis=1, keepdims=True)
        lens = jnp.broadcast_to(prmv[pl.ds(s, 1), :].astype(F32), (TOK, 8))
        labels = lax.broadcasted_iota(jnp.int32, (TOK, 8), 1).astype(F32)
        prompt = jnp.sum(jnp.where(ids_t[:, :8] == labels, lens, 0.0), axis=1, keepdims=True)
        alive = jnp.where(place >= prompt, 1.0, 0.0)
        count = jnp.sum(alive, axis=0, keepdims=True)
        live[s] = jnp.broadcast_to(alive / count, (TOK, 128))

        def one_head(h):
            cut = pl.ds(pl.multiple_of(h * HEAD_DIM, HEAD_DIM), HEAD_DIM)
            scores = lax.dot_general(
                qv[s, :, cut], kv[s, :, cut], (((1,), (1,)), ((), ())), preferred_element_type=F32
            ) / math.sqrt(HEAD_DIM)
            scores = jnp.where(allowed, scores, -jnp.inf)
            top = jnp.max(scores, axis=1, keepdims=True)
            weights = jnp.exp(scores - top)
            soft = weights / jnp.sum(weights, axis=1, keepdims=True)
            att[s, h] = soft.astype(BF16)
            att_t[s, h] = soft.T.astype(BF16)

        loop(0, 2, one_head)

    def value_grad(s, values):
        vals[...] = values

        def one_head(h):
            cut = pl.ds(pl.multiple_of(h * HEAD_DIM, HEAD_DIM), HEAD_DIM)
            attended = jnp.dot(att[s, h], vals[:, cut], preferred_element_type=F32)
            residue = attended - tv[s, :, cut].astype(F32)
            errors = (residue * live[s]).astype(BF16)
            dvals[s, :, cut] = jnp.dot(
                att_t[s, h], errors, preferred_element_type=F32
            ).astype(BF16)

        loop(0, 2, one_head)

    def rows_of(i):
        return pl.ds(pl.multiple_of(i * CROWS, CROWS), CROWS)

    def send(s, i):
        cut = pl.ds(i * CROWS, CROWS)
        return remote(
            stepped.at[s, cut], landed.at[s, cut], g_send.at[s, i], g_recv.at[s, i], peers[s]
        )

    def out_copy(n, i):
        cut = rows_of(i)
        source, target = ((wv, w_out), (mv, m_out))[n]
        return pltpu.make_async_copy(source.at[cut], target.at[0, cut], out_sem.at[n, i])

    def grad_rows(n, i, dvalues):
        lhs = x[n, :, :, rows_of(i)].reshape(TOK, CROWS)
        return lax.dot_general(lhs, dvalues, (((0,), (0,)), ((), ())), preferred_element_type=F32)

    def moment_rows(s, i):
        cut = rows_of(i)
        moment = (
            MOMENTUM_DECAY * mv[cut, :].astype(F32) + grad_rows(s, i, dvals[s])
        ).astype(BF16)
        mv[cut, :] = moment
        return moment

    def update(s, i, target):
        cut = rows_of(i)
        moment = moment_rows(s, i)
        target[cut, :] = (wv[cut, :].astype(F32) - LEARN_RATE * moment.astype(F32)).astype(BF16)

    def average(s, i):
        cut = rows_of(i)
        send(s, i).wait_recv()
        mean = (stepped[s, cut, :].astype(F32) + landed[s, cut, :].astype(F32)) * 0.5
        wv[cut, :] = mean.astype(BF16)

    def add_values(i, count=1):
        cut = pl.ds(pl.multiple_of(i * CROWS, CROWS), count * CROWS)
        total[...] += jnp.dot(
            x[1, :, :, cut].reshape(TOK, count * CROWS), wv[cut, :], preferred_element_type=F32
        )

    def first_update(i):
        update(0, i, stepped.at[0])
        send(0, i).start()

    def first_updates(k):
        first_update(2 * k)
        first_update(2 * k + 1)

    def first_gossip(i):
        average(0, i)
        if early:
            cut = rows_of(i)
            ahead = wv[cut, :].astype(F32) - (LEARN_RATE * MOMENTUM_DECAY) * mv[cut, :].astype(F32)
            stepped[1, cut, :] = ahead.astype(BF16)
            send(1, i).start()

    def first_gossip_values(i):
        first_gossip(i)
        add_values(i)

    def second_update(i):
        if early:
            update(1, i, held)
        else:
            update(1, i, stepped.at[1])
            send(1, i).start()
        out_copy(1, i).start()

    def second_gossip(i):
        if early:
            cut = rows_of(i)
            send(1, i).wait_recv()
            theirs = landed[1, cut, :].astype(F32) - LEARN_RATE * grad_rows(2, i, dvals[2])
            wv[cut, :] = ((held[cut, :].astype(F32) + theirs) * 0.5).astype(BF16)
        else:
            average(1, i)
        out_copy(0, i).start()

    def finish(i):
        for s in range(2):
            send(s, i).wait_send()
            out_copy(s, i).wait()

    if early:
        their_rows = remote(
            hid.at[0, 1], x.at[2, tp], low_send.at[0], low_recv.at[0], peers[1]
        )
        their_grad = remote(dvals.at[1], dvals.at[2], low_send.at[1], low_recv.at[1], peers[1])
    if paired or ring:
        their_rows = remote(
            hid.at[0, 1], x.at[2, tp], low_send.at[0], low_recv.at[0], partner
        )
        product = remote(dvals.at[0], dvals.at[2], low_send.at[1], low_recv.at[1], partner)

    def partner_values(between):
        stage_b(1)
        stage_c(1)
        their_rows.wait_recv()
        stage_a(2)
        stage_d(1)
        total[...] = jnp.dot(
            x[1].reshape(TOK, ROWS), stepped[0], preferred_element_type=F32
        )
        stage_b(2)
        stage_c(2)
        stage_d(2)
        dvals[0] = jnp.dot(
            x[2].reshape(TOK, ROWS), stepped[0], preferred_element_type=F32
        ).astype(BF16)
        product.start()
        between()
        product.wait_recv()
        values = ((total[...] + dvals[2].astype(F32)) * 0.5).astype(BF16)
        value_grad(1, values)

    def partner_end():
        product.wait_send()
        their_rows.wait_send()
        for s in range(3):
            stage_end(s)

    def ring_steps():
        half = CHUNKS // 2

        def both(k, body):
            body(k, 0)
            body(half + k, 1)

        def passing(n, i, way):
            cut = rows_of(i)
            source = (stepped.at[0], stepped.at[1], held)[n]
            device = peers[1 - way if n == 0 else way]
            return remote(
                source.at[cut], landed.at[n, cut], g_send.at[n, i], g_recv.at[n, i], device
            )

        def step(i, way):
            update(0, i, stepped.at[0])

        def pass_step(i, way):
            passing(0, i, way).start()

        def second(i, way):
            cut = rows_of(i)
            moment = moment_rows(1, i)
            out_copy(1, i).start()
            stepped[1, cut, :] = (
                stepped[0, cut, :].astype(F32) - (2 * LEARN_RATE) * moment.astype(F32)
            ).astype(BF16)
            passing(1, i, way).start()

        def relay(i, way):
            cut = rows_of(i)
            passing(1, i, way).wait_recv()
            held[cut, :] = (
                landed[1, cut, :].astype(F32) + stepped[0, cut, :].astype(F32)
            ).astype(BF16)
            passing(2, i, way).start()

        def weights(i, way):
            cut = rows_of(i)
            passing(0, i, way).wait_recv()
            passing(2, i, way).wait_recv()
            own = stepped[0, cut, :].astype(F32) - (2 * LEARN_RATE) * mv[cut, :].astype(F32)
            theirs = landed[0, cut, :].astype(F32) + landed[2, cut, :].astype(F32)
            wv[cut, :] = ((own + theirs) * 0.25).astype(BF16)
            out_copy(0, i).start()

        def end(i, way):
            for n in range(3):
                passing(n, i, way).wait_send()
            out_copy(0, i).wait()
            out_copy(1, i).wait()

        def each(first, last, *bodies):
            def step_both(k):
                for body in bodies:
                    both(k, body)

            loop(first, last, step_both)

        each(0, 2, step, pass_step)
        each(2, half, step)
        partner_values(lambda: each(2, half, pass_step))
        each(0, half, second)
        each(0, half, relay)
        each(0, half, weights)
        each(0, half, end)
        partner_end()

    def paired_steps():
        quarter = CHUNKS // 2
        mine = (rep % 2) * quarter
        other = quarter - mine

        def crossing(n, k):
            base = (other, mine, other, mine)[n]
            cut = rows_of(base + k)
            source, target = (
                (stepped.at[0], landed.at[0]),
                (stepped.at[1], landed.at[1]),
                (mv, held),
                (wv, landed.at[0]),
            )[n]
            m = n // 2 * quarter + k
            return remote(
                source.at[cut],
                target.at[cut],
                g_send.at[n % 2, m],
                g_recv.at[n % 2, m],
                peers[1 - n] if n < 2 else peers[1],
            )

        def weight_out(k, theirs):
            cut = rows_of((other if theirs else mine) + k)
            source = landed.at[0] if theirs else wv
            sem = out_sem.at[0, k + quarter * theirs]
            return pltpu.make_async_copy(source.at[cut], w_out.at[0, cut], sem)

        def step_for_mate(k):
            update(0, other + k, stepped.at[0])
            crossing(0, k).start()

        def step_for_chip(k):
            update(0, mine + k, stepped.at[0])
            cut = rows_of(mine + k)
            crossing(0, k).wait_recv()
            both = (stepped[0, cut, :].astype(F32) + landed[0, cut, :].astype(F32)) * 0.5
            stepped[1, cut, :] = both.astype(BF16)
            crossing(1, k).start()

        def moment_for_mate(k):
            moment_rows(1, other + k)
            crossing(2, k).start()
            out_copy(1, other + k).start()

        def moment_for_chip(k):
            moment_rows(1, mine + k)
            out_copy(1, mine + k).start()

        def weights(k):
            cut = rows_of(mine + k)
            crossing(2, k).wait_recv()
            crossing(1, k).wait_recv()
            both = stepped[1, cut, :].astype(F32) + landed[1, cut, :].astype(F32)
            moments = mv[cut, :].astype(F32) + held[cut, :].astype(F32)
            wv[cut, :] = (both * 0.5 - (0.5 * LEARN_RATE) * moments).astype(BF16)
            crossing(3, k).start()
            weight_out(k, False).start()

        def weights_of_mate(k):
            crossing(3, k).wait_recv()
            weight_out(k, True).start()

        def end(k):
            for n in range(4):
                crossing(n, k).wait_send()
            weight_out(k, False).wait()
            weight_out(k, True).wait()
            out_copy(1, mine + k).wait()
            out_copy(1, other + k).wait()

        loop(0, quarter, step_for_mate)
        loop(0, quarter, step_for_chip)
        partner_values(lambda: None)
        loop(0, quarter, moment_for_mate)
        loop(0, quarter, moment_for_chip)
        loop(0, quarter, weights)
        loop(0, quarter, weights_of_mate)
        loop(0, quarter, end)
        partner_end()

    own_load[0].wait()
    stage_a(0)
    if early or paired or ring:
        their_rows.start()
    for copy in loads[:5]:
        copy.wait()
    attention(0)
    stage_b(0)
    stage_c(0)
    own_load[1].wait()
    if lean:
        start(1, 2, 3)
    elif bit_a == 0:
        stage_a(1)
    attention(1)
    for copy in loads[5:]:
        copy.wait()
    stage_d(0)
    if lean:
        start(1, 0, 1, 4, 5)
        their_rows.wait_recv()
        start(2, 2, 3)
    elif bit_a > 0:
        stage_a(1)

    values = jnp.dot(
        x[0].reshape(TOK, ROWS), wv[...], preferred_element_type=F32
    ).astype(BF16)
    value_grad(0, values)
    if paired:
        paired_steps()
        return
    if ring:
        ring_steps()
        return
    if bit_a == 0:
        stage_b(1)
    if bit_a == 0:
        loop(0, CHUNKS // 2, first_updates)
    else:
        loop(0, CHUNKS, first_update)
    total[...] = jnp.zeros((TOK, COLS), F32)
    if bit_a == 0:
        stage_c(1)
        loop(0, CHUNKS, first_gossip)
        stage_d(1)
        add_values(0, CHUNKS)
    else:
        stage_b(1)
        stage_c(1)
        if lean:
            start(2, 0, 1, 4, 5)
        elif early:
            their_rows.wait_recv()
            stage_a(2)
        loop(0, 4, first_gossip)
        stage_d(1)
        add_values(0, 4)
        if early:
            stage_b(2)
        loop(4, 6, first_gossip_values)
        if early:
            stage_c(2)
        loop(6, CHUNKS, first_gossip_values)

    value_grad(1, total[...].astype(BF16))
    if early:
        their_grad.start()
    loop(0, CHUNKS, second_update)
    if early:
        stage_d(2)
        their_grad.wait_recv()
    loop(0, CHUNKS, second_gossip)
    loop(0, CHUNKS, finish)
    stage_end(0)
    stage_end(1)
    if early:
        stage_end(2)
        their_rows.wait_send()
        their_grad.wait_send()


def fused(bit, *operands):
    hid, qry, key, tea, seg, prm, wgt, mom = operands
    any_space = pl.BlockSpec(memory_space=pl.ANY)
    dma = pltpu.SemaphoreType.DMA
    return pl.pallas_call(
        functools.partial(kernel, bit, (bit + 1) % LEVELS),
        out_shape=(
            jax.ShapeDtypeStruct(wgt.shape, BF16),
            jax.ShapeDtypeStruct(mom.shape, BF16),
        ),
        in_specs=[any_space] * 8,
        out_specs=(any_space, any_space),
        scratch_shapes=[
            pltpu.VMEM((3, TP, SHARD, ROWS), BF16),
            pltpu.VMEM((2, TOK, COLS), BF16),
            pltpu.VMEM((2, TOK, COLS), BF16),
            pltpu.VMEM((2, TOK, COLS), BF16),
            pltpu.VMEM((2, TOK), jnp.int32),
            pltpu.VMEM((2, 8), jnp.int32),
            pltpu.VMEM((ROWS, COLS), BF16),
            pltpu.VMEM((ROWS, COLS), BF16),
            pltpu.VMEM((2, ROWS, COLS), BF16),
            pltpu.VMEM((3, ROWS, COLS), BF16),
            pltpu.VMEM((ROWS, COLS), BF16),
            pltpu.VMEM((2, 2, TOK, TOK), BF16),
            pltpu.VMEM((2, 2, TOK, TOK), BF16),
            pltpu.VMEM((2, TOK, 128), F32),
            pltpu.VMEM((TOK, COLS), BF16),
            pltpu.VMEM((3, TOK, COLS), BF16),
            pltpu.VMEM((TOK, COLS), F32),
            dma((9,)),
            dma((3, 14)),
            dma((3, 14)),
            dma((3, CHUNKS)),
            dma((3, CHUNKS)),
            dma((2,)),
            dma((2,)),
            dma((2, CHUNKS)),
        ],
        compiler_params=pltpu.CompilerParams(
            collective_id=bit, has_side_effects=True, vmem_limit_bytes=56 * 1024 * 1024
        ),
        name=f"gossip_{bit}",
    )(*operands)


def per_device(hid, qry, key, tea, seg, prm, gossip_step, wgt, mom):
    bit = gossip_step[0] % LEVELS
    branches = [functools.partial(fused, level) for level in range(LEVELS)]
    return lax.switch(bit, branches, hid, qry, key, tea, seg, prm, wgt, mom)


def solution(mesh):
    in_specs = (
        P("rep", None, "tp", None),
        P("rep", None, None, "tp"),
        P("rep", None, None, "tp"),
        P("rep", None, None, "tp"),
        P("rep", None, None),
        P("rep", None, None),
        P(),
        P("rep", None, "tp"),
        P("rep", None, "tp"),
    )
    out_specs = (P("rep", None, "tp"), P("rep", None, "tp"))
    return jax.shard_map(
        per_device, mesh=mesh, in_specs=in_specs, out_specs=out_specs, check_vma=False
    )
```

```python
import functools
import math

import jax
import jax.numpy as jnp
from jax import lax
from jax.experimental import pallas as pl
from jax.experimental.pallas import tpu as pltpu
from jax.sharding import PartitionSpec as P

HEAD_DIM = 128
LEARN_RATE = 0.1
MOMENTUM_DECAY = 0.9
LEVELS = 6
REPS = 1 << LEVELS
TOK = 256
ROWS = 2048
COLS = 256
TP = 8
SHARD = TOK // TP
HALF = ROWS // 2
CHUNKS = 8
CROWS = ROWS // CHUNKS
F32 = jnp.float32
BF16 = jnp.bfloat16
MESH = pl.DeviceIdType.MESH


def remote(src, dst, send, recv, device):
    return pltpu.make_async_remote_copy(
        src_ref=src, dst_ref=dst, send_sem=send, recv_sem=recv, device_id=device, device_id_type=MESH
    )


def partner_of(rep, bit):
    size = 1 << bit
    return rep + size * (1 - 2 * ((rep // size) % 2))


def kernel(
    bit_a, bit_b,
    hid, qry, key, tea, seg, prm, wgt, mom,
    w_out, m_out,
    x, qv, kv, tv, segv, prmv, wv, mv, stepped, landed, held, att, att_t, live, vals, dvals, total,
    load_sem, x_send, x_recv, g_send, g_recv, low_send, low_recv, out_sem,
):
    early = bit_a in (1, 2, 3)
    paired = bit_b == 0
    ring = bit_a == 4
    lean = bit_a == 1
    rep = lax.axis_index("rep")
    tp = lax.axis_index("tp")
    row = (tp // 4) * 4
    right = row + (tp + 1) % 4
    left = row + (tp + 3) % 4
    cross = (tp + 4) % 8
    far = row + (tp + 2) % 4
    cross_right = (right + 4) % 8
    cross_left = (left + 4) % 8
    to_right = (rep, right)
    to_left = (rep, left)
    to_cross = (rep, cross)
    partner = (partner_of(rep, bit_a), tp)
    peers = (partner, (partner_of(rep, bit_b), tp))
    if ring:
        peers = (((rep + (1 << bit_a)) % REPS, tp), ((rep + REPS - (1 << bit_a)) % REPS, tp))

    own_load = [pltpu.make_async_copy(hid.at[0, s], x.at[s, tp], load_sem.at[s]) for s in range(2)]
    loads = [
        pltpu.make_async_copy(seg.at[0], segv, load_sem.at[2]),
        pltpu.make_async_copy(prm.at[0], prmv, load_sem.at[3]),
        pltpu.make_async_copy(qry.at[0], qv, load_sem.at[4]),
        pltpu.make_async_copy(key.at[0], kv, load_sem.at[5]),
        pltpu.make_async_copy(tea.at[0], tv, load_sem.at[6]),
        pltpu.make_async_copy(wgt.at[0], wv, load_sem.at[7]),
        pltpu.make_async_copy(mom.at[0], mv, load_sem.at[8]),
    ]
    for copy in own_load + loads:
        copy.start()

    barrier = pltpu.get_barrier_semaphore()
    for device in (to_right, to_left, to_cross) + peers:
        pl.semaphore_signal(barrier, inc=1, device_id=device, device_id_type=MESH)
    pl.semaphore_wait(barrier, 5)

    route = (
        (tp, to_right, 0),
        (tp, to_left, 1),
        (tp, to_cross, 0),
        (tp, to_cross, 1),
        (tp, to_right, 1),
        (tp, to_left, 0),
        (left, to_right, 0),
        (right, to_left, 1),
        (cross, to_right, 0),
        (cross, to_left, 0),
        (cross, to_right, 1),
        (cross, to_left, 1),
        (far, to_cross, 0),
        (far, to_cross, 1),
    )

    lean_route = route[:12] + ((cross_left, to_right, 0), (cross_right, to_left, 1))

    def hop(s, n):
        slot, device, half = (lean_route if lean and s else route)[n]
        part = x.at[s, slot, :, pl.ds(half * HALF, HALF)]
        return remote(part, part, x_send.at[s, n], x_recv.at[s, n], device)

    def start(s, *hops):
        for n in hops:
            hop(s, n).start()

    def stage_a(s):
        start(s, 2, 0, 1, 3, 4, 5)

    def stage_b(s):
        for arrived, onward in ((0, (6,)), (1, (7,)), (2, (8, 9)), (3, (10, 11))):
            hop(s, arrived).wait_recv()
            start(s, *onward)

    def stage_c(s):
        for arrived, onward in ((8, 12), (11, 13)) if lean and s else ((6, 12), (7, 13)):
            hop(s, arrived).wait_recv()
            start(s, onward)

    def stage_d(s):
        for n in (4, 5, 6, 7, 9, 10, 12, 13) if lean and s else (4, 5, 8, 9, 10, 11, 12, 13):
            hop(s, n).wait_recv()

    def stage_end(s):
        for n in range(14):
            hop(s, n).wait_send()

    def loop(first, last, body):
        def step(i, carry):
            body(i)
            return carry

        lax.fori_loop(first, last, step, 0)

    def attention(s):
        ids = jnp.broadcast_to(segv[pl.ds(s, 1), :].astype(F32), (TOK, TOK))
        ids_t = ids.T
        rows = lax.broadcasted_iota(jnp.int32, (TOK, TOK), 0)
        columns = lax.broadcasted_iota(jnp.int32, (TOK, TOK), 1)
        same = ids == ids_t
        allowed = same & (columns <= rows)
        place = jnp.sum(jnp.where(same & (columns < rows), 1.0, 0.0), axis=1, keepdims=True)
        lens = jnp.broadcast_to(prmv[pl.ds(s, 1), :].astype(F32), (TOK, 8))
        labels = lax.broadcasted_iota(jnp.int32, (TOK, 8), 1).astype(F32)
        prompt = jnp.sum(jnp.where(ids_t[:, :8] == labels, lens, 0.0), axis=1, keepdims=True)
        alive = jnp.where(place >= prompt, 1.0, 0.0)
        count = jnp.sum(alive, axis=0, keepdims=True)
        live[s] = jnp.broadcast_to(alive / count, (TOK, 128))

        def one_head(h):
            cut = pl.ds(pl.multiple_of(h * HEAD_DIM, HEAD_DIM), HEAD_DIM)
            scores = lax.dot_general(
                qv[s, :, cut], kv[s, :, cut], (((1,), (1,)), ((), ())), preferred_element_type=F32
            ) / math.sqrt(HEAD_DIM)
            scores = jnp.where(allowed, scores, -jnp.inf)
            top = jnp.max(scores, axis=1, keepdims=True)
            weights = jnp.exp(scores - top)
            soft = weights / jnp.sum(weights, axis=1, keepdims=True)
            att[s, h] = soft.astype(BF16)
            att_t[s, h] = soft.T.astype(BF16)

        loop(0, 2, one_head)

    def value_grad(s, values):
        vals[...] = values

        def one_head(h):
            cut = pl.ds(pl.multiple_of(h * HEAD_DIM, HEAD_DIM), HEAD_DIM)
            attended = jnp.dot(att[s, h], vals[:, cut], preferred_element_type=F32)
            residue = attended - tv[s, :, cut].astype(F32)
            errors = (residue * live[s]).astype(BF16)
            dvals[s, :, cut] = jnp.dot(
                att_t[s, h], errors, preferred_element_type=F32
            ).astype(BF16)

        loop(0, 2, one_head)

    def rows_of(i):
        return pl.ds(pl.multiple_of(i * CROWS, CROWS), CROWS)

    def send(s, i):
        cut = pl.ds(i * CROWS, CROWS)
        return remote(
            stepped.at[s, cut], landed.at[s, cut], g_send.at[s, i], g_recv.at[s, i], peers[s]
        )

    def out_copy(n, i):
        cut = rows_of(i)
        source, target = ((wv, w_out), (mv, m_out))[n]
        return pltpu.make_async_copy(source.at[cut], target.at[0, cut], out_sem.at[n, i])

    def grad_rows(n, i, dvalues):
        lhs = x[n, :, :, rows_of(i)].reshape(TOK, CROWS)
        return lax.dot_general(lhs, dvalues, (((0,), (0,)), ((), ())), preferred_element_type=F32)

    def moment_rows(s, i):
        cut = rows_of(i)
        moment = (
            MOMENTUM_DECAY * mv[cut, :].astype(F32) + grad_rows(s, i, dvals[s])
        ).astype(BF16)
        mv[cut, :] = moment
        return moment

    def update(s, i, target):
        cut = rows_of(i)
        moment = moment_rows(s, i)
        target[cut, :] = (wv[cut, :].astype(F32) - LEARN_RATE * moment.astype(F32)).astype(BF16)

    def average(s, i):
        cut = rows_of(i)
        send(s, i).wait_recv()
        mean = (stepped[s, cut, :].astype(F32) + landed[s, cut, :].astype(F32)) * 0.5
        wv[cut, :] = mean.astype(BF16)

    def add_values(i, count=1):
        cut = pl.ds(pl.multiple_of(i * CROWS, CROWS), count * CROWS)
        total[...] += jnp.dot(
            x[1, :, :, cut].reshape(TOK, count * CROWS), wv[cut, :], preferred_element_type=F32
        )

    def first_update(i):
        update(0, i, stepped.at[0])
        send(0, i).start()

    def first_updates(k):
        first_update(2 * k)
        first_update(2 * k + 1)

    def first_gossip(i):
        average(0, i)
        if early:
            cut = rows_of(i)
            ahead = wv[cut, :].astype(F32) - (LEARN_RATE * MOMENTUM_DECAY) * mv[cut, :].astype(F32)
            stepped[1, cut, :] = ahead.astype(BF16)
            send(1, i).start()

    def first_gossip_values(i):
        first_gossip(i)
        add_values(i)

    def second_update(i):
        if early:
            update(1, i, held)
        else:
            update(1, i, stepped.at[1])
            send(1, i).start()
        out_copy(1, i).start()

    def second_gossip(i):
        if early:
            cut = rows_of(i)
            send(1, i).wait_recv()
            theirs = landed[1, cut, :].astype(F32) - LEARN_RATE * grad_rows(2, i, dvals[2])
            wv[cut, :] = ((held[cut, :].astype(F32) + theirs) * 0.5).astype(BF16)
        else:
            average(1, i)
        out_copy(0, i).start()

    def finish(i):
        for s in range(2):
            send(s, i).wait_send()
            out_copy(s, i).wait()

    if early:
        their_rows = remote(
            hid.at[0, 1], x.at[2, tp], low_send.at[0], low_recv.at[0], peers[1]
        )
        their_grad = remote(dvals.at[1], dvals.at[2], low_send.at[1], low_recv.at[1], peers[1])
    if paired or ring:
        their_rows = remote(
            hid.at[0, 1], x.at[2, tp], low_send.at[0], low_recv.at[0], partner
        )
        product = remote(dvals.at[0], dvals.at[2], low_send.at[1], low_recv.at[1], partner)

    def partner_values(between):
        stage_b(1)
        stage_c(1)
        their_rows.wait_recv()
        stage_a(2)
        stage_d(1)
        total[...] = jnp.dot(
            x[1].reshape(TOK, ROWS), stepped[0], preferred_element_type=F32
        )
        stage_b(2)
        stage_c(2)
        stage_d(2)
        dvals[0] = jnp.dot(
            x[2].reshape(TOK, ROWS), stepped[0], preferred_element_type=F32
        ).astype(BF16)
        product.start()
        between()
        product.wait_recv()
        values = ((total[...] + dvals[2].astype(F32)) * 0.5).astype(BF16)
        value_grad(1, values)

    def partner_end():
        product.wait_send()
        their_rows.wait_send()
        for s in range(3):
            stage_end(s)

    def ring_steps():
        half = CHUNKS // 2

        def both(k, body):
            body(k, 0)
            body(half + k, 1)

        def passing(n, i, way):
            cut = rows_of(i)
            source = (stepped.at[0], stepped.at[1], held)[n]
            device = peers[1 - way if n == 0 else way]
            return remote(
                source.at[cut], landed.at[n, cut], g_send.at[n, i], g_recv.at[n, i], device
            )

        def step(i, way):
            update(0, i, stepped.at[0])

        def pass_step(i, way):
            passing(0, i, way).start()

        def second(i, way):
            cut = rows_of(i)
            moment = moment_rows(1, i)
            out_copy(1, i).start()
            stepped[1, cut, :] = (
                stepped[0, cut, :].astype(F32) - (2 * LEARN_RATE) * moment.astype(F32)
            ).astype(BF16)
            passing(1, i, way).start()

        def relay(i, way):
            cut = rows_of(i)
            passing(1, i, way).wait_recv()
            held[cut, :] = (
                landed[1, cut, :].astype(F32) + stepped[0, cut, :].astype(F32)
            ).astype(BF16)
            passing(2, i, way).start()

        def weights(i, way):
            cut = rows_of(i)
            passing(0, i, way).wait_recv()
            passing(2, i, way).wait_recv()
            own = stepped[0, cut, :].astype(F32) - (2 * LEARN_RATE) * mv[cut, :].astype(F32)
            theirs = landed[0, cut, :].astype(F32) + landed[2, cut, :].astype(F32)
            wv[cut, :] = ((own + theirs) * 0.25).astype(BF16)
            out_copy(0, i).start()

        def end(i, way):
            for n in range(3):
                passing(n, i, way).wait_send()
            out_copy(0, i).wait()
            out_copy(1, i).wait()

        def each(first, last, *bodies):
            def step_both(k):
                for body in bodies:
                    both(k, body)

            loop(first, last, step_both)

        each(0, 2, step, pass_step)
        each(2, half, step)
        partner_values(lambda: each(2, half, pass_step))
        each(0, half, second)
        each(0, half, relay)
        each(0, half, weights)
        each(0, half, end)
        partner_end()

    def paired_steps():
        quarter = CHUNKS // 2
        mine = (rep % 2) * quarter
        other = quarter - mine

        def crossing(n, k):
            base = (other, mine, other, mine)[n]
            cut = rows_of(base + k)
            source, target = (
                (stepped.at[0], landed.at[0]),
                (stepped.at[1], landed.at[1]),
                (mv, held),
                (wv, landed.at[0]),
            )[n]
            m = n // 2 * quarter + k
            return remote(
                source.at[cut],
                target.at[cut],
                g_send.at[n % 2, m],
                g_recv.at[n % 2, m],
                peers[1 - n] if n < 2 else peers[1],
            )

        def weight_out(k, theirs):
            cut = rows_of((other if theirs else mine) + k)
            source = landed.at[0] if theirs else wv
            sem = out_sem.at[0, k + quarter * theirs]
            return pltpu.make_async_copy(source.at[cut], w_out.at[0, cut], sem)

        def step_for_mate(k):
            update(0, other + k, stepped.at[0])
            crossing(0, k).start()

        def step_for_chip(k):
            update(0, mine + k, stepped.at[0])
            cut = rows_of(mine + k)
            crossing(0, k).wait_recv()
            both = (stepped[0, cut, :].astype(F32) + landed[0, cut, :].astype(F32)) * 0.5
            stepped[1, cut, :] = both.astype(BF16)
            crossing(1, k).start()

        def moment_for_mate(k):
            moment_rows(1, other + k)
            crossing(2, k).start()
            out_copy(1, other + k).start()

        def moment_for_chip(k):
            moment_rows(1, mine + k)
            out_copy(1, mine + k).start()

        def weights(k):
            cut = rows_of(mine + k)
            crossing(2, k).wait_recv()
            crossing(1, k).wait_recv()
            both = stepped[1, cut, :].astype(F32) + landed[1, cut, :].astype(F32)
            moments = mv[cut, :].astype(F32) + held[cut, :].astype(F32)
            wv[cut, :] = (both * 0.5 - (0.5 * LEARN_RATE) * moments).astype(BF16)
            crossing(3, k).start()
            weight_out(k, False).start()

        def weights_of_mate(k):
            crossing(3, k).wait_recv()
            weight_out(k, True).start()

        def end(k):
            for n in range(4):
                crossing(n, k).wait_send()
            weight_out(k, False).wait()
            weight_out(k, True).wait()
            out_copy(1, mine + k).wait()
            out_copy(1, other + k).wait()

        loop(0, quarter, step_for_mate)
        loop(0, quarter, step_for_chip)
        partner_values(lambda: None)
        loop(0, quarter, moment_for_mate)
        loop(0, quarter, moment_for_chip)
        loop(0, quarter, weights)
        loop(0, quarter, weights_of_mate)
        loop(0, quarter, end)
        partner_end()

    own_load[0].wait()
    stage_a(0)
    if early or paired or ring:
        their_rows.start()
    stage_b(0)
    stage_c(0)
    own_load[1].wait()
    if lean:
        start(1, 2, 3)
    elif bit_a == 0:
        stage_a(1)
    for copy in loads:
        copy.wait()
    loop(0, 2, attention)
    stage_d(0)
    if lean:
        start(1, 0, 1, 4, 5)
        their_rows.wait_recv()
        start(2, 2, 3)
    elif bit_a > 0:
        stage_a(1)

    values = jnp.dot(
        x[0].reshape(TOK, ROWS), wv[...], preferred_element_type=F32
    ).astype(BF16)
    value_grad(0, values)
    if paired:
        paired_steps()
        return
    if ring:
        ring_steps()
        return
    if bit_a == 0:
        stage_b(1)
    if bit_a == 0:
        loop(0, CHUNKS // 2, first_updates)
    else:
        loop(0, CHUNKS, first_update)
    total[...] = jnp.zeros((TOK, COLS), F32)
    if bit_a == 0:
        stage_c(1)
        loop(0, CHUNKS, first_gossip)
        stage_d(1)
        add_values(0, CHUNKS)
    else:
        stage_b(1)
        stage_c(1)
        if lean:
            start(2, 0, 1, 4, 5)
        elif early:
            their_rows.wait_recv()
            stage_a(2)
        loop(0, 4, first_gossip)
        stage_d(1)
        add_values(0, 4)
        if early:
            stage_b(2)
        loop(4, 6, first_gossip_values)
        if early:
            stage_c(2)
        loop(6, CHUNKS, first_gossip_values)

    value_grad(1, total[...].astype(BF16))
    if early:
        their_grad.start()
    loop(0, CHUNKS, second_update)
    if early:
        stage_d(2)
        their_grad.wait_recv()
    loop(0, CHUNKS, second_gossip)
    loop(0, CHUNKS, finish)
    stage_end(0)
    stage_end(1)
    if early:
        stage_end(2)
        their_rows.wait_send()
        their_grad.wait_send()


def fused(bit, *operands):
    hid, qry, key, tea, seg, prm, wgt, mom = operands
    any_space = pl.BlockSpec(memory_space=pl.ANY)
    dma = pltpu.SemaphoreType.DMA
    return pl.pallas_call(
        functools.partial(kernel, bit, (bit + 1) % LEVELS),
        out_shape=(
            jax.ShapeDtypeStruct(wgt.shape, BF16),
            jax.ShapeDtypeStruct(mom.shape, BF16),
        ),
        in_specs=[any_space] * 8,
        out_specs=(any_space, any_space),
        scratch_shapes=[
            pltpu.VMEM((3, TP, SHARD, ROWS), BF16),
            pltpu.VMEM((2, TOK, COLS), BF16),
            pltpu.VMEM((2, TOK, COLS), BF16),
            pltpu.VMEM((2, TOK, COLS), BF16),
            pltpu.VMEM((2, TOK), jnp.int32),
            pltpu.VMEM((2, 8), jnp.int32),
            pltpu.VMEM((ROWS, COLS), BF16),
            pltpu.VMEM((ROWS, COLS), BF16),
            pltpu.VMEM((2, ROWS, COLS), BF16),
            pltpu.VMEM((3, ROWS, COLS), BF16),
            pltpu.VMEM((ROWS, COLS), BF16),
            pltpu.VMEM((2, 2, TOK, TOK), BF16),
            pltpu.VMEM((2, 2, TOK, TOK), BF16),
            pltpu.VMEM((2, TOK, 128), F32),
            pltpu.VMEM((TOK, COLS), BF16),
            pltpu.VMEM((3, TOK, COLS), BF16),
            pltpu.VMEM((TOK, COLS), F32),
            dma((9,)),
            dma((3, 14)),
            dma((3, 14)),
            dma((3, CHUNKS)),
            dma((3, CHUNKS)),
            dma((2,)),
            dma((2,)),
            dma((2, CHUNKS)),
        ],
        compiler_params=pltpu.CompilerParams(
            collective_id=bit, has_side_effects=True, vmem_limit_bytes=56 * 1024 * 1024
        ),
        name=f"gossip_{bit}",
    )(*operands)


def per_device(hid, qry, key, tea, seg, prm, gossip_step, wgt, mom):
    bit = gossip_step[0] % LEVELS
    branches = [functools.partial(fused, level) for level in range(LEVELS)]
    return lax.switch(bit, branches, hid, qry, key, tea, seg, prm, wgt, mom)


def solution(mesh):
    in_specs = (
        P("rep", None, "tp", None),
        P("rep", None, None, "tp"),
        P("rep", None, None, "tp"),
        P("rep", None, None, "tp"),
        P("rep", None, None),
        P("rep", None, None),
        P(),
        P("rep", None, "tp"),
        P("rep", None, "tp"),
    )
    out_specs = (P("rep", None, "tp"), P("rep", None, "tp"))
    return jax.shard_map(
        per_device, mesh=mesh, in_specs=in_specs, out_specs=out_specs, check_vma=False
    )
```

```python
import functools
import math

import jax
import jax.numpy as jnp
from jax import lax
from jax.experimental import pallas as pl
from jax.experimental.pallas import tpu as pltpu
from jax.sharding import PartitionSpec as P

HEAD_DIM = 128
LEARN_RATE = 0.1
MOMENTUM_DECAY = 0.9
LEVELS = 6
REPS = 1 << LEVELS
TOK = 256
ROWS = 2048
COLS = 256
TP = 8
SHARD = TOK // TP
HALF = ROWS // 2
CHUNKS = 8
CROWS = ROWS // CHUNKS
F32 = jnp.float32
BF16 = jnp.bfloat16
MESH = pl.DeviceIdType.MESH


def remote(src, dst, send, recv, device):
    return pltpu.make_async_remote_copy(
        src_ref=src, dst_ref=dst, send_sem=send, recv_sem=recv, device_id=device, device_id_type=MESH
    )


def partner_of(rep, bit):
    size = 1 << bit
    return rep + size * (1 - 2 * ((rep // size) % 2))


def kernel(
    bit_a, bit_b,
    hid, qry, key, tea, seg, prm, wgt, mom,
    w_out, m_out,
    x, qv, kv, tv, segv, prmv, wv, mv, stepped, landed, held, att, att_t, live, vals, dvals, total,
    load_sem, x_send, x_recv, g_send, g_recv, low_send, low_recv, out_sem,
):
    early = bit_a in (1, 2, 3)
    paired = bit_b == 0
    ring = bit_a == 4
    lean = bit_a == 1
    rep = lax.axis_index("rep")
    tp = lax.axis_index("tp")
    row = (tp // 4) * 4
    right = row + (tp + 1) % 4
    left = row + (tp + 3) % 4
    cross = (tp + 4) % 8
    far = row + (tp + 2) % 4
    cross_right = (right + 4) % 8
    cross_left = (left + 4) % 8
    to_right = (rep, right)
    to_left = (rep, left)
    to_cross = (rep, cross)
    partner = (partner_of(rep, bit_a), tp)
    peers = (partner, (partner_of(rep, bit_b), tp))
    if ring:
        peers = (((rep + (1 << bit_a)) % REPS, tp), ((rep + REPS - (1 << bit_a)) % REPS, tp))

    own_load = [pltpu.make_async_copy(hid.at[0, s], x.at[s, tp], load_sem.at[s]) for s in range(2)]
    loads = [
        pltpu.make_async_copy(seg.at[0], segv, load_sem.at[2]),
        pltpu.make_async_copy(prm.at[0], prmv, load_sem.at[3]),
        pltpu.make_async_copy(qry.at[0], qv, load_sem.at[4]),
        pltpu.make_async_copy(key.at[0], kv, load_sem.at[5]),
        pltpu.make_async_copy(tea.at[0], tv, load_sem.at[6]),
        pltpu.make_async_copy(wgt.at[0], wv, load_sem.at[7]),
        pltpu.make_async_copy(mom.at[0], mv, load_sem.at[8]),
    ]
    barrier = pltpu.get_barrier_semaphore()
    for device in (to_right, to_left, to_cross) + peers:
        pl.semaphore_signal(barrier, inc=1, device_id=device, device_id_type=MESH)
    for copy in own_load + loads:
        copy.start()
    pl.semaphore_wait(barrier, 5)

    route = (
        (tp, to_right, 0),
        (tp, to_left, 1),
        (tp, to_cross, 0),
        (tp, to_cross, 1),
        (tp, to_right, 1),
        (tp, to_left, 0),
        (left, to_right, 0),
        (right, to_left, 1),
        (cross, to_right, 0),
        (cross, to_left, 0),
        (cross, to_right, 1),
        (cross, to_left, 1),
        (far, to_cross, 0),
        (far, to_cross, 1),
    )

    lean_route = route[:12] + ((cross_left, to_right, 0), (cross_right, to_left, 1))

    def hop(s, n):
        slot, device, half = (lean_route if lean and s else route)[n]
        cut = pl.ds(half * HALF, HALF)
        part = x.at[s, slot, :, cut]
        source = hid.at[0, s, :, cut] if n < 6 and s < 2 else part
        return remote(source, part, x_send.at[s, n], x_recv.at[s, n], device)

    def start(s, *hops):
        for n in hops:
            hop(s, n).start()

    def stage_a(s):
        start(s, 2, 0, 1, 3, 4, 5)

    def stage_b(s):
        for arrived, onward in ((0, (6,)), (1, (7,)), (2, (8, 9)), (3, (10, 11))):
            hop(s, arrived).wait_recv()
            start(s, *onward)

    def stage_c(s):
        for arrived, onward in ((8, 12), (11, 13)) if lean and s else ((6, 12), (7, 13)):
            hop(s, arrived).wait_recv()
            start(s, onward)

    def stage_d(s):
        for n in (4, 5, 6, 7, 9, 10, 12, 13) if lean and s else (4, 5, 8, 9, 10, 11, 12, 13):
            hop(s, n).wait_recv()

    def stage_end(s):
        for n in range(14):
            hop(s, n).wait_send()

    def loop(first, last, body):
        def step(i, carry):
            body(i)
            return carry

        lax.fori_loop(first, last, step, 0)

    def attention(s):
        ids = jnp.broadcast_to(segv[pl.ds(s, 1), :].astype(F32), (TOK, TOK))
        ids_t = ids.T
        rows = lax.broadcasted_iota(jnp.int32, (TOK, TOK), 0)
        columns = lax.broadcasted_iota(jnp.int32, (TOK, TOK), 1)
        same = ids == ids_t
        allowed = same & (columns <= rows)
        place = jnp.sum(jnp.where(same & (columns < rows), 1.0, 0.0), axis=1, keepdims=True)
        lens = jnp.broadcast_to(prmv[pl.ds(s, 1), :].astype(F32), (TOK, 8))
        labels = lax.broadcasted_iota(jnp.int32, (TOK, 8), 1).astype(F32)
        prompt = jnp.sum(jnp.where(ids_t[:, :8] == labels, lens, 0.0), axis=1, keepdims=True)
        alive = jnp.where(place >= prompt, 1.0, 0.0)
        count = jnp.sum(alive, axis=0, keepdims=True)
        live[s] = jnp.broadcast_to(alive / count, (TOK, 128))

        def one_head(h):
            cut = pl.ds(pl.multiple_of(h * HEAD_DIM, HEAD_DIM), HEAD_DIM)
            scores = lax.dot_general(
                qv[s, :, cut], kv[s, :, cut], (((1,), (1,)), ((), ())), preferred_element_type=F32
            ) / math.sqrt(HEAD_DIM)
            scores = jnp.where(allowed, scores, -jnp.inf)
            top = jnp.max(scores, axis=1, keepdims=True)
            weights = jnp.exp(scores - top)
            soft = weights / jnp.sum(weights, axis=1, keepdims=True)
            att[s, h] = soft.astype(BF16)
            att_t[s, h] = soft.T.astype(BF16)

        loop(0, 2, one_head)

    def value_grad(s, values):
        vals[...] = values

        def one_head(h):
            cut = pl.ds(pl.multiple_of(h * HEAD_DIM, HEAD_DIM), HEAD_DIM)
            attended = jnp.dot(att[s, h], vals[:, cut], preferred_element_type=F32)
            residue = attended - tv[s, :, cut].astype(F32)
            errors = (residue * live[s]).astype(BF16)
            dvals[s, :, cut] = jnp.dot(
                att_t[s, h], errors, preferred_element_type=F32
            ).astype(BF16)

        loop(0, 2, one_head)

    def rows_of(i):
        return pl.ds(pl.multiple_of(i * CROWS, CROWS), CROWS)

    def send(s, i):
        cut = pl.ds(i * CROWS, CROWS)
        return remote(
            stepped.at[s, cut], landed.at[s, cut], g_send.at[s, i], g_recv.at[s, i], peers[s]
        )

    def out_copy(n, i):
        cut = rows_of(i)
        source, target = ((wv, w_out), (mv, m_out))[n]
        return pltpu.make_async_copy(source.at[cut], target.at[0, cut], out_sem.at[n, i])

    def grad_rows(n, i, dvalues):
        lhs = x[n, :, :, rows_of(i)].reshape(TOK, CROWS)
        return lax.dot_general(lhs, dvalues, (((0,), (0,)), ((), ())), preferred_element_type=F32)

    def moment_rows(s, i):
        cut = rows_of(i)
        moment = (
            MOMENTUM_DECAY * mv[cut, :].astype(F32) + grad_rows(s, i, dvals[s])
        ).astype(BF16)
        mv[cut, :] = moment
        return moment

    def update(s, i, target):
        cut = rows_of(i)
        moment = moment_rows(s, i)
        target[cut, :] = (wv[cut, :].astype(F32) - LEARN_RATE * moment.astype(F32)).astype(BF16)

    def average(s, i):
        cut = rows_of(i)
        send(s, i).wait_recv()
        mean = (stepped[s, cut, :].astype(F32) + landed[s, cut, :].astype(F32)) * 0.5
        wv[cut, :] = mean.astype(BF16)

    def add_values(i, count=1):
        cut = pl.ds(pl.multiple_of(i * CROWS, CROWS), count * CROWS)
        total[...] += jnp.dot(
            x[1, :, :, cut].reshape(TOK, count * CROWS), wv[cut, :], preferred_element_type=F32
        )

    def first_update(i):
        update(0, i, stepped.at[0])
        send(0, i).start()

    def first_updates(k):
        first_update(2 * k)
        first_update(2 * k + 1)

    def first_gossip(i):
        average(0, i)
        if early:
            cut = rows_of(i)
            ahead = wv[cut, :].astype(F32) - (LEARN_RATE * MOMENTUM_DECAY) * mv[cut, :].astype(F32)
            stepped[1, cut, :] = ahead.astype(BF16)
            send(1, i).start()

    def first_gossip_values(i):
        first_gossip(i)
        add_values(i)

    def second_update(i):
        if early:
            update(1, i, held)
        else:
            update(1, i, stepped.at[1])
            send(1, i).start()
        out_copy(1, i).start()

    def second_gossip(i):
        if early:
            cut = rows_of(i)
            send(1, i).wait_recv()
            theirs = landed[1, cut, :].astype(F32) - LEARN_RATE * grad_rows(2, i, dvals[2])
            wv[cut, :] = ((held[cut, :].astype(F32) + theirs) * 0.5).astype(BF16)
        else:
            average(1, i)
        out_copy(0, i).start()

    def finish(i):
        for s in range(2):
            send(s, i).wait_send()
            out_copy(s, i).wait()

    if early:
        their_rows = remote(
            hid.at[0, 1], x.at[2, tp], low_send.at[0], low_recv.at[0], peers[1]
        )
        their_grad = remote(dvals.at[1], dvals.at[2], low_send.at[1], low_recv.at[1], peers[1])
    if paired or ring:
        their_rows = remote(
            hid.at[0, 1], x.at[2, tp], low_send.at[0], low_recv.at[0], partner
        )
        product = remote(dvals.at[0], dvals.at[2], low_send.at[1], low_recv.at[1], partner)

    def partner_values(between):
        stage_b(1)
        stage_c(1)
        their_rows.wait_recv()
        stage_a(2)
        stage_d(1)
        total[...] = jnp.dot(
            x[1].reshape(TOK, ROWS), stepped[0], preferred_element_type=F32
        )
        stage_b(2)
        stage_c(2)
        stage_d(2)
        dvals[0] = jnp.dot(
            x[2].reshape(TOK, ROWS), stepped[0], preferred_element_type=F32
        ).astype(BF16)
        product.start()
        between()
        product.wait_recv()
        values = ((total[...] + dvals[2].astype(F32)) * 0.5).astype(BF16)
        value_grad(1, values)

    def partner_end():
        product.wait_send()
        their_rows.wait_send()
        for s in range(3):
            stage_end(s)

    def ring_steps():
        half = CHUNKS // 2

        def both(k, body):
            body(k, 0)
            body(half + k, 1)

        def passing(n, i, way):
            cut = rows_of(i)
            source = (stepped.at[0], stepped.at[1], held)[n]
            device = peers[1 - way if n == 0 else way]
            return remote(
                source.at[cut], landed.at[n, cut], g_send.at[n, i], g_recv.at[n, i], device
            )

        def step(i, way):
            update(0, i, stepped.at[0])

        def pass_step(i, way):
            passing(0, i, way).start()

        def second(i, way):
            cut = rows_of(i)
            moment = moment_rows(1, i)
            out_copy(1, i).start()
            stepped[1, cut, :] = (
                stepped[0, cut, :].astype(F32) - (2 * LEARN_RATE) * moment.astype(F32)
            ).astype(BF16)
            passing(1, i, way).start()

        def relay(i, way):
            cut = rows_of(i)
            passing(1, i, way).wait_recv()
            held[cut, :] = (
                landed[1, cut, :].astype(F32) + stepped[0, cut, :].astype(F32)
            ).astype(BF16)
            passing(2, i, way).start()

        def weights(i, way):
            cut = rows_of(i)
            passing(0, i, way).wait_recv()
            passing(2, i, way).wait_recv()
            own = stepped[0, cut, :].astype(F32) - (2 * LEARN_RATE) * mv[cut, :].astype(F32)
            theirs = landed[0, cut, :].astype(F32) + landed[2, cut, :].astype(F32)
            wv[cut, :] = ((own + theirs) * 0.25).astype(BF16)
            out_copy(0, i).start()

        def end(i, way):
            for n in range(3):
                passing(n, i, way).wait_send()
            out_copy(0, i).wait()
            out_copy(1, i).wait()

        def each(first, last, *bodies):
            def step_both(k):
                for body in bodies:
                    both(k, body)

            loop(first, last, step_both)

        each(0, 2, step, pass_step)
        each(2, half, step)
        partner_values(lambda: each(2, half, pass_step))
        each(0, half, second)
        each(0, half, relay)
        each(0, half, weights)
        each(0, half, end)
        partner_end()

    def paired_steps():
        quarter = CHUNKS // 2
        mine = (rep % 2) * quarter
        other = quarter - mine

        def crossing(n, k):
            base = (other, mine, other, mine)[n]
            cut = rows_of(base + k)
            source, target = (
                (stepped.at[0], landed.at[0]),
                (stepped.at[1], landed.at[1]),
                (mv, held),
                (wv, landed.at[0]),
            )[n]
            m = n // 2 * quarter + k
            return remote(
                source.at[cut],
                target.at[cut],
                g_send.at[n % 2, m],
                g_recv.at[n % 2, m],
                peers[1 - n] if n < 2 else peers[1],
            )

        def weight_out(k, theirs):
            cut = rows_of((other if theirs else mine) + k)
            source = landed.at[0] if theirs else wv
            sem = out_sem.at[0, k + quarter * theirs]
            return pltpu.make_async_copy(source.at[cut], w_out.at[0, cut], sem)

        def step_for_mate(k):
            update(0, other + k, stepped.at[0])
            crossing(0, k).start()

        def step_for_chip(k):
            update(0, mine + k, stepped.at[0])
            cut = rows_of(mine + k)
            crossing(0, k).wait_recv()
            both = (stepped[0, cut, :].astype(F32) + landed[0, cut, :].astype(F32)) * 0.5
            stepped[1, cut, :] = both.astype(BF16)
            crossing(1, k).start()

        def moment_for_mate(k):
            moment_rows(1, other + k)
            crossing(2, k).start()
            out_copy(1, other + k).start()

        def moment_for_chip(k):
            moment_rows(1, mine + k)
            out_copy(1, mine + k).start()

        def weights(k):
            cut = rows_of(mine + k)
            crossing(2, k).wait_recv()
            crossing(1, k).wait_recv()
            both = stepped[1, cut, :].astype(F32) + landed[1, cut, :].astype(F32)
            moments = mv[cut, :].astype(F32) + held[cut, :].astype(F32)
            wv[cut, :] = (both * 0.5 - (0.5 * LEARN_RATE) * moments).astype(BF16)
            crossing(3, k).start()
            weight_out(k, False).start()

        def weights_of_mate(k):
            crossing(3, k).wait_recv()
            weight_out(k, True).start()

        def end(k):
            for n in range(4):
                crossing(n, k).wait_send()
            weight_out(k, False).wait()
            weight_out(k, True).wait()
            out_copy(1, mine + k).wait()
            out_copy(1, other + k).wait()

        loop(0, quarter, step_for_mate)
        loop(0, quarter, step_for_chip)
        partner_values(lambda: None)
        loop(0, quarter, moment_for_mate)
        loop(0, quarter, moment_for_chip)
        loop(0, quarter, weights)
        loop(0, quarter, weights_of_mate)
        loop(0, quarter, end)
        partner_end()

    stage_a(0)
    if early or paired or ring:
        their_rows.start()
    stage_b(0)
    stage_c(0)
    if lean:
        start(1, 2, 3)
    elif bit_a == 0:
        stage_a(1)
    for copy in own_load + loads:
        copy.wait()
    loop(0, 2, attention)
    stage_d(0)
    if lean:
        start(1, 0, 1, 4, 5)
        their_rows.wait_recv()
        start(2, 2, 3)
    elif bit_a > 0:
        stage_a(1)

    values = jnp.dot(
        x[0].reshape(TOK, ROWS), wv[...], preferred_element_type=F32
    ).astype(BF16)
    value_grad(0, values)
    if paired:
        paired_steps()
        return
    if ring:
        ring_steps()
        return
    if bit_a == 0:
        stage_b(1)
    if bit_a == 0:
        loop(0, CHUNKS // 2, first_updates)
    else:
        loop(0, CHUNKS, first_update)
    total[...] = jnp.zeros((TOK, COLS), F32)
    if bit_a == 0:
        stage_c(1)
        loop(0, CHUNKS, first_gossip)
        stage_d(1)
        add_values(0, CHUNKS)
    else:
        stage_b(1)
        stage_c(1)
        if lean:
            start(2, 0, 1, 4, 5)
        elif early:
            their_rows.wait_recv()
            stage_a(2)
        loop(0, 4, first_gossip)
        stage_d(1)
        add_values(0, 4)
        if early:
            stage_b(2)
        loop(4, 6, first_gossip_values)
        if early:
            stage_c(2)
        loop(6, CHUNKS, first_gossip_values)

    value_grad(1, total[...].astype(BF16))
    if early:
        their_grad.start()
    loop(0, CHUNKS, second_update)
    if early:
        stage_d(2)
        their_grad.wait_recv()
    loop(0, CHUNKS, second_gossip)
    loop(0, CHUNKS, finish)
    stage_end(0)
    stage_end(1)
    if early:
        stage_end(2)
        their_rows.wait_send()
        their_grad.wait_send()


def fused(bit, *operands):
    hid, qry, key, tea, seg, prm, wgt, mom = operands
    any_space = pl.BlockSpec(memory_space=pl.ANY)
    dma = pltpu.SemaphoreType.DMA
    return pl.pallas_call(
        functools.partial(kernel, bit, (bit + 1) % LEVELS),
        out_shape=(
            jax.ShapeDtypeStruct(wgt.shape, BF16),
            jax.ShapeDtypeStruct(mom.shape, BF16),
        ),
        in_specs=[any_space] * 8,
        out_specs=(any_space, any_space),
        scratch_shapes=[
            pltpu.VMEM((3, TP, SHARD, ROWS), BF16),
            pltpu.VMEM((2, TOK, COLS), BF16),
            pltpu.VMEM((2, TOK, COLS), BF16),
            pltpu.VMEM((2, TOK, COLS), BF16),
            pltpu.VMEM((2, TOK), jnp.int32),
            pltpu.VMEM((2, 8), jnp.int32),
            pltpu.VMEM((ROWS, COLS), BF16),
            pltpu.VMEM((ROWS, COLS), BF16),
            pltpu.VMEM((2, ROWS, COLS), BF16),
            pltpu.VMEM((3, ROWS, COLS), BF16),
            pltpu.VMEM((ROWS, COLS), BF16),
            pltpu.VMEM((2, 2, TOK, TOK), BF16),
            pltpu.VMEM((2, 2, TOK, TOK), BF16),
            pltpu.VMEM((2, TOK, 128), F32),
            pltpu.VMEM((TOK, COLS), BF16),
            pltpu.VMEM((3, TOK, COLS), BF16),
            pltpu.VMEM((TOK, COLS), F32),
            dma((9,)),
            dma((3, 14)),
            dma((3, 14)),
            dma((3, CHUNKS)),
            dma((3, CHUNKS)),
            dma((2,)),
            dma((2,)),
            dma((2, CHUNKS)),
        ],
        compiler_params=pltpu.CompilerParams(
            collective_id=bit, has_side_effects=True, vmem_limit_bytes=56 * 1024 * 1024
        ),
        name=f"gossip_{bit}",
    )(*operands)


def per_device(hid, qry, key, tea, seg, prm, gossip_step, wgt, mom):
    bit = gossip_step[0] % LEVELS
    branches = [functools.partial(fused, level) for level in range(LEVELS)]
    return lax.switch(bit, branches, hid, qry, key, tea, seg, prm, wgt, mom)


def solution(mesh):
    in_specs = (
        P("rep", None, "tp", None),
        P("rep", None, None, "tp"),
        P("rep", None, None, "tp"),
        P("rep", None, None, "tp"),
        P("rep", None, None),
        P("rep", None, None),
        P(),
        P("rep", None, "tp"),
        P("rep", None, "tp"),
    )
    out_specs = (P("rep", None, "tp"), P("rep", None, "tp"))
    return jax.shard_map(
        per_device, mesh=mesh, in_specs=in_specs, out_specs=out_specs, check_vma=False
    )
```
